128 devices in a mesh: tm: 8 (over y, z_lo), space: 16 (over z_hi, x, core).
Axes of the slice: x: 4, y: 4, z: 4 (z_hi: 2, z_lo: 2; z = z_hi * 2 + z_lo), core: 2. Of those that a mesh axis runs over, the one named last changes fastest.
Arguments:
- video_query: bfloat16 [48, 16, 64, 1536], P('tm', 'space'), may hold values from -8 to 8
- video_key: bfloat16 [48, 16, 64, 1536], P('tm', 'space'), may hold values from -8 to 8
- video_value: bfloat16 [48, 16, 64, 1536], P('tm', 'space'), may hold values from -6 to 6
- text_query: bfloat16 [256, 1536], P(('tm', 'space')), may hold values from -8 to 8
- text_key: bfloat16 [256, 1536], P(('tm', 'space')), may hold values from -8 to 8
- text_value: bfloat16 [256, 1536], P(('tm', 'space')), may hold values from -6 to 6
- window_lists: int32 [8, 16, 27], P('tm'), may hold values from -1 to 127, as said below
- valid_columns: int32 [8], replicated, may hold values from 2 to 8, as said below
- video_weight: bfloat16 [1536, 3072], replicated, may hold values from -0.15625 to 0.15625
- text_weight: bfloat16 [1536, 3072], replicated, may hold values from -0.15625 to 0.15625
Outputs:
- video_output: bfloat16 [8, 16, 1, 384, 3072], P('tm', 'space')
- text_output: bfloat16 [256, 3072], P(('tm', 'space'))
The draws below stay inside these ranges and needn't reach their ends.
Inputs may be any that keep to these rules, and one draw needn't show every extreme that they name: window_lists[t, b * 8 + w] names, each once and in any order, the tile t * 16 + b * 8 + w itself and some of the tiles t2 * 16 + b2 * 8 + w2 with t2 within one of t, b2 within one of b and w2 within one of w (0 <= b2 < 2, 0 <= w2 < 8); its other entries are -1. `valid_columns`: 8 in every tile column except column 7.
All inputs are finite; a program needn't handle non-finite values.
Results may differ from the reference program's by a relative error of at most 0.0085.
Values may be sent and summed in bfloat16 or wider, within the bound.
No kernel may reach another device: no remote copies, remote signals or barrier semaphores. Data moves between devices by JAX's collectives and lax.ppermute only.
A program may use at most 192 MiB of HBM per device.

```python
import jax
import jax.numpy as jnp
from jax import lax

WIDTH = 3072
HEADS = 12
HD = 128
TXT = 256
TF = 6
TR = 8
TC = 8
SW = 8
BANDS = 2
WIN = 27
F = 1536
NT = 8
SLAB = 16
FRAMES = 48
ROWS = 16
COLS = 64
N_SPACE = 16


def query_shaped(key, shape, spread_scale):
    base = spread_scale * jax.random.normal(key, shape, jnp.float32)
    return jnp.clip(base, -8.0, 8.0).astype(jnp.bfloat16)


def key_like(key, shape, spread_scale):
    base = spread_scale * jax.random.normal(key, shape, jnp.float32)
    return jnp.clip(base, -8.0, 8.0).astype(jnp.bfloat16)


def draw_video_query(key, part):
    shape = (FRAMES, ROWS, COLS, F)
    key = jax.random.fold_in(key, 3)
    return query_shaped(key, shape, 1.4)


def draw_video_key(key, part):
    shape = (FRAMES, ROWS, COLS, F)
    key = jax.random.fold_in(key, 5)
    return key_like(key, shape, 1.4)


def draw_text_query(key, part):
    shape = (TXT, F)
    key = jax.random.fold_in(key, 11)
    return query_shaped(key, shape, 2.5)


def draw_text_key(key, part):
    shape = (TXT, F)
    key = jax.random.fold_in(key, 13)
    return key_like(key, shape, 1.4)


def draw_window_lists(key, part):
    key = jax.random.fold_in(key, 7)
    slab_index = jnp.arange(NT, dtype=jnp.int32)[:, None, None]
    place_index = jnp.arange(SLAB, dtype=jnp.int32)[None, :, None]
    offsets = jnp.arange(WIN, dtype=jnp.int32)[None, None, :]
    moment = slab_index + offsets // 9 - 1
    band = place_index // SW + offsets // 3 % 3 - 1
    column = place_index % SW + offsets % 3 - 1
    inside = (moment >= 0) & (moment < NT) & (band >= 0) & (band < BANDS) & (column >= 0) & (column < SW)
    idents = moment * SLAB + band * SW + column
    coin_flips = jax.random.randint(jax.random.fold_in(key, 1), (NT, SLAB, 1), 0, 2)
    dropped = jax.random.randint(jax.random.fold_in(key, 2), (NT, SLAB, 1), 0, WIN)
    removed = (coin_flips == 1) & (offsets == dropped) & (offsets != 13)
    entries = jnp.where(inside & jnp.logical_not(removed), idents, -1)
    rank_keys = jax.random.randint(jax.random.fold_in(key, 3), (NT, SLAB, WIN), 0, 1 << 20) * WIN + offsets
    shuffle = jnp.argsort(rank_keys, axis=-1, stable=True)
    return jnp.take_along_axis(entries, shuffle, axis=-1).astype(jnp.int32)


def draw_valid_columns(key, part):
    key = jax.random.fold_in(key, 9)
    place_index = jnp.arange(SW, dtype=jnp.int32)
    ragged = jax.random.randint(key, (SW,), 2, TC)
    return jnp.where(place_index == SW - 1, ragged, TC).astype(jnp.int32)


def levels(rng, shape, cuts, low, top_value):
    gain = 1.0
    for dim, parts in cuts:
        heights = jax.random.uniform(jax.random.fold_in(jax.random.fold_in(rng, 6), dim), (parts,), jnp.float32, low / len(cuts), top_value / len(cuts))
        gain = gain * jnp.repeat(jnp.exp(heights), shape[dim] // parts).reshape((-1,) + (1,) * (len(shape) - 1 - dim))
    return gain


def centred(own_key, dims, deviation, bound, split=(), kind=jnp.bfloat16):
    array = deviation * jax.random.normal(own_key, dims, jnp.float32)
    if split:
        array = array * levels(own_key, dims, split, -0.22, 0.18)
    return jnp.clip(array, -bound, bound).astype(kind)


def setup_inputs(seed: int = 0) -> dict:
    key_list = jax.random.split(jax.random.key(seed), 11)
    return {
        "video_query": draw_video_query(jax.random.fold_in(key_list[10], 71), 0),
        "video_key": draw_video_key(jax.random.fold_in(key_list[10], 71), 0),
        "video_value": centred(key_list[2], (FRAMES, ROWS, COLS, F), 1.0, 6.0, ((0, 8), (1, 16))),
        "text_query": draw_text_query(jax.random.fold_in(key_list[10], 71), 0),
        "text_key": draw_text_key(jax.random.fold_in(key_list[10], 71), 0),
        "text_value": centred(key_list[5], (TXT, F), 1.0, 6.0, ((0, 128),)),
        "window_lists": draw_window_lists(jax.random.fold_in(key_list[10], 71), 0),
        "valid_columns": draw_valid_columns(jax.random.fold_in(key_list[10], 71), 0),
        "video_weight": centred(key_list[8], (F, WIDTH), F ** -0.5, 0.15625),
        "text_weight": centred(key_list[9], (F, WIDTH), F ** -0.5, 0.15625),
    }


def to_tiles(raster):
    slab_count = raster.shape[0] // TF
    band_count = raster.shape[1] // TR
    across = raster.shape[2] // TC
    feature_vectors = raster.shape[3]
    blocks = raster.reshape(slab_count, TF, band_count, TR, across, TC, feature_vectors)
    blocks = blocks.transpose(0, 2, 4, 1, 3, 5, 6)
    return blocks.reshape(slab_count, band_count * across, TF * TR * TC, feature_vectors)


def rounded(weights):
    return lax.optimization_barrier(weights.astype(jnp.bfloat16)).astype(jnp.float32)


def reference(video_query, video_key, video_value, text_query, text_key, text_value, window_lists, valid_columns, video_weight, text_weight):
    scaling = HD ** -0.5
    tiles_all = NT * SLAB
    tile_size = TF * TR * TC
    kept = 9 * min(BANDS, 3)
    query_tiles = to_tiles(video_query).reshape(tiles_all, tile_size, F)
    key_tiles = to_tiles(video_key).reshape(tiles_all, tile_size, F)
    value_tiles = to_tiles(video_value).reshape(tiles_all, tile_size, F)
    column = jnp.arange(tile_size, dtype=jnp.int32) % TC
    tile_column = jnp.arange(SLAB, dtype=jnp.int32) % SW
    limits = jnp.sum(jnp.where(tile_column[:, None] == jnp.arange(SW, dtype=jnp.int32)[None, :], valid_columns[None, :], 0), axis=1)
    usable = column[None, :] < limits[:, None]
    usable = jnp.broadcast_to(usable[None], (NT, SLAB, tile_size)).reshape(tiles_all, tile_size)
    window_ids = window_lists.reshape(tiles_all, WIN)
    order = jnp.argsort((window_ids < 0).astype(jnp.int32), axis=1, stable=True)
    window_ids = jnp.take_along_axis(window_ids, order, axis=1)[:, :kept]
    text_keys = text_key.astype(jnp.float32).reshape(TXT, HEADS, HD)
    text_values = text_value.astype(jnp.float32).reshape(TXT, HEADS, HD)

    def one_tile(inputs):
        queries, idents, own_usable = inputs
        chosen = jnp.maximum(idents, 0).astype(jnp.int32)
        window_keys = key_tiles[chosen].astype(jnp.float32).reshape(kept * tile_size, HEADS, HD)
        values = value_tiles[chosen].astype(jnp.float32).reshape(kept * tile_size, HEADS, HD)
        allowed = ((idents >= 0)[:, None] & usable[chosen]).reshape(kept * tile_size)
        queries = queries.astype(jnp.float32).reshape(tile_size, HEADS, HD)
        near_scores = jnp.einsum('qhd,khd->hqk', queries, window_keys) * scaling
        near_scores = jnp.where(allowed[None, None, :], near_scores, -jnp.inf)
        textual = jnp.einsum('qhd,khd->hqk', queries, text_keys) * scaling
        highest = jnp.maximum(jnp.max(near_scores, axis=2), jnp.max(textual, axis=2))
        near_weights = jnp.where(allowed[None, None, :], jnp.exp(near_scores - highest[:, :, None]), 0.0)
        text_weights = jnp.exp(textual - highest[:, :, None])
        totals = jnp.sum(near_weights, axis=2) + jnp.sum(text_weights, axis=2)
        summed = jnp.einsum('hqk,khd->qhd', rounded(near_weights), values)
        summed = summed + jnp.einsum('hqk,khd->qhd', rounded(text_weights), text_values)
        attended = summed / totals.T[:, :, None]
        attended = jnp.where(own_usable[:, None, None], attended, 0.0)
        return attended.reshape(tile_size, F).astype(jnp.bfloat16)

    video_attn = lax.map(one_tile, (query_tiles, window_ids, usable))
    projected = jnp.dot(video_attn.reshape(tiles_all * tile_size, F), video_weight, preferred_element_type=jnp.float32)
    group_count = N_SPACE // SW
    per_block = BANDS // group_count
    projected = projected.astype(jnp.bfloat16).reshape(NT, group_count, per_block, SW, tile_size, WIDTH)
    video_output = projected.transpose(0, 3, 1, 2, 4, 5).reshape(NT, N_SPACE, per_block, tile_size, WIDTH)

    all_keys = key_tiles.reshape(tiles_all * tile_size, F)
    all_values = value_tiles.reshape(tiles_all * tile_size, F)
    all_usable = usable.reshape(tiles_all * tile_size)

    def text_head(head_index):
        offset = head_index * HD
        queries = lax.dynamic_slice_in_dim(text_query, offset, HD, 1)
        video_keys = lax.dynamic_slice_in_dim(all_keys, offset, HD, 1)
        video_value_rows = lax.dynamic_slice_in_dim(all_values, offset, HD, 1)
        own_keys = lax.dynamic_slice_in_dim(text_key, offset, HD, 1)
        own_values = lax.dynamic_slice_in_dim(text_value, offset, HD, 1)
        video_scores = jnp.dot(queries, video_keys.T, preferred_element_type=jnp.float32) * scaling
        video_scores = jnp.where(all_usable[None, :], video_scores, -jnp.inf)
        text_scores = jnp.dot(queries, own_keys.T, preferred_element_type=jnp.float32) * scaling
        highest = jnp.maximum(jnp.max(video_scores, axis=1), jnp.max(text_scores, axis=1))
        video_weights = jnp.where(all_usable[None, :], jnp.exp(video_scores - highest[:, None]), 0.0)
        text_weights = jnp.exp(text_scores - highest[:, None])
        totals = jnp.sum(video_weights, axis=1) + jnp.sum(text_weights, axis=1)
        summed = jnp.dot(video_weights.astype(jnp.bfloat16), video_value_rows, preferred_element_type=jnp.float32)
        summed = summed + jnp.dot(text_weights.astype(jnp.bfloat16), own_values, preferred_element_type=jnp.float32)
        return summed / totals[:, None]

    text_attn = lax.map(text_head, jnp.arange(HEADS, dtype=jnp.int32))
    text_attn = text_attn.transpose(1, 0, 2).reshape(TXT, F).astype(jnp.bfloat16)
    text_output = jnp.dot(text_attn, text_weight, preferred_element_type=jnp.float32).astype(jnp.bfloat16)
    return video_output, text_output
```

```python
import functools
import math

import jax
import jax.numpy as jnp
from jax import lax
from jax.experimental import pallas as pl
from jax.experimental.pallas import tpu as pltpu
from jax.sharding import PartitionSpec as P

HD = 128
TF = 6
TC = 8
TILE = 384
CELL = 2 * TILE
GW = 384
GH = GW // HD
TXT = 256
AXES = ("tm", "space")
SCALE = HD**-0.5 * math.log2(math.e)
MASKED = -1e30
CONTRACT_LAST = (((1,), (1,)), ((), ()))


def device(y, z, x, c):
    return (2 * y + z % 2) * 16 + 8 * (z // 2) + 2 * x + c


PLACES = [(y, z, x, c) for y in range(4) for z in range(4) for x in range(4) for c in range(2)]
PLANES = [
    [device(y, z, x, c) for z in range(4) for x in range(4)] for y in range(4) for c in range(2)
]


def route(target):
    pairs = []
    for place in PLACES:
        goal = target(*place)
        if goal is not None:
            pairs.append((device(*place), device(*goal)))
    return pairs


def in_time(steps):
    def target(y, z, x, c):
        moment = 2 * y + c + steps
        return (moment // 2, z, x, moment % 2) if 0 <= moment < 8 else None

    return route(target)


def in_columns(steps):
    return route(lambda y, z, x, c: (y, z, x + steps, c) if 0 <= x + steps < 4 else None)


def to_owner(turn):
    def target(y, z, x, c):
        tile = (z + turn) % 4
        return (y, 2 * (x // 2) + c, 2 * (x % 2) + tile // 2, tile % 2)

    return route(target)


OTHER_CORE = route(lambda y, z, x, c: (y, z, x, 1 - c))


def along_y(steps):
    return route(lambda y, z, x, c: ((y + steps) % 4, z, x, c))


def send(value, pairs):
    return lax.ppermute(value, AXES, pairs)


def spread(value):
    return lax.all_to_all(
        value, AXES, split_axis=0, concat_axis=0, tiled=True, axis_index_groups=PLANES
    )


def attend_kernel(rows, lane, groups, has_text, has_state, final, *refs):
    refs = list(refs)
    valid_ref = refs.pop(0)
    q_ref = refs.pop(0)
    step = pl.program_id(1)
    lanes = lax.broadcasted_iota(jnp.int32, (rows, HD), 1)
    hot = jnp.where(lanes == (step if lane is None else lane), 1.0, 0.0).astype(jnp.bfloat16)
    query = jnp.concatenate([q_ref[0], hot], axis=1)
    if has_state:
        old_sum, old_mark = refs.pop(0)[0], refs.pop(0)[0]
        peak = old_mark[:, :1]
        total = jnp.concatenate(
            [old_sum, jnp.broadcast_to(old_mark[:, HD // 2 : HD // 2 + 1], (rows, HD))], axis=1
        )
    else:
        peak, total = None, None
    blocks = []
    if has_text:
        k_ref, v_ref, b_ref = refs.pop(0), refs.pop(0), refs.pop(0)
        blocks.append((k_ref.at[0], v_ref.at[0], b_ref))
    for cells in groups:
        k_ref, v_ref, b_ref = refs.pop(0), refs.pop(0), refs.pop(0)
        for i in range(cells):
            blocks.append((k_ref.at[0, i], v_ref.at[0, i], b_ref.at[0, i]))
    for keys, values, bias in blocks:
        count = keys.shape[0]
        wide_keys = jnp.concatenate([keys[...], bias[...]], axis=1)
        wide_values = jnp.concatenate([values[...], jnp.ones((count, HD), jnp.bfloat16)], axis=1)
        scores = lax.dot_general(
            query, wide_keys, CONTRACT_LAST, preferred_element_type=jnp.float32
        )
        top = jnp.max(scores, axis=1, keepdims=True)
        if peak is not None:
            top = jnp.maximum(top, peak)
        weights = jnp.exp2((scores - top) * SCALE).astype(jnp.bfloat16)
        part = jnp.dot(weights, wide_values, preferred_element_type=jnp.float32)
        if peak is not None:
            part = part + total * jnp.exp2((peak - top) * SCALE)
        peak, total = top, part
    if final:
        (out_ref,) = refs
        row = lax.broadcasted_iota(jnp.int32, (rows, HD), 0)
        usable = row % TC < valid_ref[step // 2]
        out_ref[0] = jnp.where(usable, total[:, :HD] / total[:, HD:], 0.0).astype(jnp.bfloat16)
    else:
        sum_ref, mark_ref = refs
        sum_ref[0] = total[:, :HD]
        mark_ref[0] = jnp.where(
            lanes < HD // 2, jnp.broadcast_to(peak, (rows, HD)), total[:, HD:]
        )


def attend(name, valid, queries, state, text, groups, lane=None, final=False):
    steps, rows, width = queries.shape
    heads = width // HD
    tall = pl.BlockSpec((1, rows, HD), lambda h, i: (i, 0, h))
    specs = [pl.BlockSpec(memory_space=pltpu.SMEM), tall]
    operands = [valid, queries]
    if state is not None:
        specs += [tall, tall]
        operands += list(state)
    keys = 0
    if text is not None:
        text_keys, text_values, text_bias = text
        specs += [
            pl.BlockSpec((1, TXT, HD), lambda h, i: (1, 0, h)),
            pl.BlockSpec((1, TXT, HD), lambda h, i: (2, 0, h)),
            pl.BlockSpec((TXT, HD), lambda h, i: (0, 0)),
        ]
        operands += [text_keys, text_values, text_bias]
        keys += TXT
    counts = []
    for cells, bias, sided in groups:
        number = 1 if sided else cells.shape[1]
        counts.append(number)
        keys += number * CELL
        if sided:
            for kind in range(2):
                specs.append(
                    pl.BlockSpec(
                        (1, 1, CELL, HD),
                        functools.partial(lambda kind, h, i: (i // 2, kind, 0, h), kind),
                    )
                )
            specs.append(pl.BlockSpec((1, 1, CELL, HD), lambda h, i: (0, i // 2, 0, 0)))
        else:
            for kind in range(2):
                specs.append(
                    pl.BlockSpec(
                        (1, number, CELL, HD),
                        functools.partial(lambda kind, h, i: (kind, 0, 0, h), kind),
                    )
                )
            specs.append(pl.BlockSpec((1, number, CELL, HD), lambda h, i: (0, 0, 0, 0)))
        operands += [cells, cells, bias[None]]
    if final:
        out_shape = jax.ShapeDtypeStruct((steps, rows, width), jnp.bfloat16)
        out_specs = tall
    else:
        out_shape = [jax.ShapeDtypeStruct((steps, rows, width), jnp.float32)] * 2
        out_specs = [tall, tall]
    scores = steps * heads * rows * keys
    return pl.pallas_call(
        functools.partial(
            attend_kernel, rows, lane, counts, text is not None, state is not None, final
        ),
        grid=(heads, steps),
        in_specs=specs,
        out_specs=out_specs,
        out_shape=out_shape,
        compiler_params=pltpu.CompilerParams(vmem_limit_bytes=48 * 2**20),
        cost_estimate=pl.CostEstimate(
            flops=scores * 4 * 256, bytes_accessed=2 * keys * width * 2, transcendentals=scores
        ),
        name=name,
    )(*operands)


def shards(
    video_query,
    video_key,
    video_value,
    text_query,
    text_key,
    text_value,
    window_lists,
    valid_columns,
    video_weight,
    text_weight,
):
    tm, space = lax.axis_index("tm"), lax.axis_index("space")
    y, zl = tm // 2, tm % 2
    zh, x, c = space // 8, space // 2 % 4, space % 2
    moment = 2 * y + c
    even_core = c == 0

    def chunks(raster):
        cut = raster.reshape(TF, 4, 2 * TC, 4, GW).transpose(3, 1, 0, 2, 4)
        return cut.reshape(16, TF * 2 * TC, GW)

    def merged(mine, other, axis):
        return jnp.stack(
            [jnp.where(even_core, mine, other), jnp.where(even_core, other, mine)], axis=axis
        )

    text_rows = jnp.concatenate([text_query, text_key, text_value], axis=0)
    text_rows = text_rows.reshape(6, 4, GW).transpose(1, 0, 2)
    lists = jnp.pad(window_lists.astype(jnp.bfloat16).reshape(-1), (0, 2 * GW - 16 * 27))
    extras = jnp.concatenate(
        [text_rows, jnp.broadcast_to(lists.reshape(1, 2, GW), (4, 2, GW))], axis=1
    )
    extras = jnp.broadcast_to(extras[:, None], (4, 4, 8, GW)).reshape(16, 8, GW)
    first = spread(jnp.concatenate([chunks(video_key), chunks(video_value), extras], axis=1))
    second = spread(chunks(video_query))

    pieces = first[:, : 4 * TF * TC].reshape(2, 2, 4, 2, TF, 2, TC, GW)
    mine = lax.dynamic_index_in_dim(pieces, c, 1, keepdims=False)
    other = send(lax.dynamic_index_in_dim(pieces, 1 - c, 1, keepdims=False), OTHER_CORE)
    own = merged(mine, other, 2).transpose(3, 5, 0, 4, 1, 2, 6, 7).reshape(2, 2, CELL, GW)

    text_mine = first[:, 4 * TF * TC : 4 * TF * TC + 6]
    text_both = merged(text_mine, send(text_mine, OTHER_CORE), 0)
    turns = [send(text_both, along_y(steps)) for steps in (3, 2, 1)] + [text_both]
    turned = jnp.stack(turns + turns)
    text_all = lax.dynamic_slice_in_dim(turned, (3 - y) % 4, 4, 0)
    text_all = text_all.reshape(4, 2, 2, 2, 4, 3, 2, GW).transpose(5, 0, 3, 2, 4, 1, 6, 7)
    text_all = text_all.reshape(3, TXT, GW)

    query_pieces = second.reshape(2, 2, 4, TF, 2, TC, GW)
    query_mine = lax.dynamic_index_in_dim(query_pieces, c, 1, keepdims=False)
    query_other = send(
        lax.dynamic_index_in_dim(query_pieces, 1 - c, 1, keepdims=False), OTHER_CORE
    )
    queries = merged(query_mine, query_other, 2).transpose(4, 0, 3, 1, 2, 5, 6)
    queries = queries.reshape(4, TILE, GW)

    past = send(own, in_time(1))
    future = send(own, in_time(-1))
    sides = jnp.stack([send(own[:, 1], in_columns(1)), send(own[:, 0], in_columns(-1))])
    past_sides = send(sides, in_time(1))
    future_sides = send(sides, in_time(-1))

    got_lists = lax.dynamic_index_in_dim(first, 4 * c, 0, keepdims=False)[4 * TF * TC + 6 :]
    got_lists = got_lists.reshape(-1)[: 16 * 27].reshape(2, 8, 27).astype(jnp.int32)
    tile_lists = lax.dynamic_slice_in_dim(got_lists, 2 * x, 2, 1).transpose(1, 0, 2).reshape(4, 27)
    key_moment = moment + jnp.arange(-1, 2, dtype=jnp.int32)[:, None, None]
    key_column = 2 * x + jnp.arange(-1, 3, dtype=jnp.int32)[None, :, None]
    key_band = jnp.arange(2, dtype=jnp.int32)[None, None, :]
    inside = (key_moment >= 0) & (key_moment < 8) & (key_column >= 0) & (key_column < 8)
    idents = jnp.where(inside, 16 * key_moment + 8 * key_band + key_column, -2)
    listed = jnp.any(idents[..., None, None] == tile_lists, axis=-1)
    places = jnp.arange(8, dtype=jnp.int32)
    columns = 2 * x + jnp.arange(-1, 3, dtype=jnp.int32)
    valid = jnp.sum(
        jnp.where(places[None, :] == columns[:, None], valid_columns[None, :], 0), axis=1
    )
    fine = places[None, :] < valid[:, None]
    listed = jnp.concatenate([listed, jnp.ones((3, 4, 2, 1), bool)], axis=3)
    listed = jnp.pad(listed, ((0, 0), (0, 0), (0, 0), (0, HD - 5)))
    allowed = listed[:, :, :, None, None, :] & fine[None, :, None, None, :, None]
    bias = jnp.where(allowed, 0.0, MASKED).astype(jnp.bfloat16)
    bias = jnp.broadcast_to(bias, (3, 4, 2, TILE // TC, TC, HD)).reshape(3, 4, CELL, HD)
    near_bias = bias[:, 1:3]
    side_bias = jnp.stack([bias[:, 0], bias[:, 3]], axis=1)
    share = jnp.arange(TXT, dtype=jnp.int32)[:, None] // 8
    text_lane = jnp.arange(HD, dtype=jnp.int32)[None, :] == 4
    text_bias = jnp.where(text_lane & (share != 8 * y + 4 * c + x), MASKED, 0.0)
    text_bias = text_bias.astype(jnp.bfloat16)

    own_valid = valid[1:3]
    text = (text_all, text_all, text_bias)
    text_sum, text_mark = attend(
        "text_queries",
        own_valid,
        text_all[:1],
        None,
        text,
        [(own, near_bias[1], False)],
        lane=4,
    )
    text_parts = jnp.concatenate([text_sum[0], text_mark[0]], axis=1).reshape(128, 2, 2 * GW)
    text_parts = lax.all_to_all(text_parts, AXES, split_axis=0, concat_axis=0, tiled=True)
    text_parts = text_parts.reshape(4, 2, 2, 4, 2, 2, 2, GH, HD)
    text_sums = text_parts[..., 0, :, :]
    text_peaks = text_parts[..., 1, :, :1]
    text_totals = text_parts[..., 1, :, HD // 2 : HD // 2 + 1]
    text_top = jnp.max(text_peaks, axis=(0, 3, 4), keepdims=True)
    factors = jnp.exp2((text_peaks - text_top) * SCALE)
    text_attn = jnp.sum(text_sums * factors, axis=(0, 3, 4)) / jnp.sum(
        text_totals * factors, axis=(0, 3, 4)
    )
    text_attn = text_attn.transpose(2, 1, 0, 3, 4).reshape(2, 4 * GW).astype(jnp.bfloat16)
    text_output = jnp.dot(text_attn, text_weight, preferred_element_type=jnp.float32)
    text_output = text_output.astype(jnp.bfloat16)

    state = attend("own_cells", own_valid, queries, None, text, [(own, near_bias[1], False)])
    state = attend(
        "time_cells",
        own_valid,
        queries,
        state,
        None,
        [(past, near_bias[0], False), (future, near_bias[2], False)],
    )
    attended = attend(
        "side_cells",
        own_valid,
        queries,
        state,
        None,
        [
            (sides, side_bias[1], True),
            (past_sides, side_bias[0], True),
            (future_sides, side_bias[2], True),
        ],
        final=True,
    )

    z = 2 * zh + zl
    arrived = [
        send(lax.dynamic_index_in_dim(attended, (z + turn) % 4, 0, keepdims=False), to_owner(turn))
        for turn in (3, 2, 1, 0)
    ]
    ordered = jnp.stack(arrived + arrived)
    tile = 2 * (x % 2) + c
    ordered = lax.dynamic_slice_in_dim(ordered, (3 - tile) % 4, 4, 0)
    video_attn = ordered.transpose(1, 0, 2).reshape(TILE, 4 * GW)
    video_output = jnp.dot(video_attn, video_weight, preferred_element_type=jnp.float32)
    video_output = video_output.astype(jnp.bfloat16).reshape(1, 1, 1, TILE, -1)
    return (video_output, text_output)


def solution(mesh):
    in_specs = (
        P("tm", "space", None, None),
        P("tm", "space", None, None),
        P("tm", "space", None, None),
        P(("tm", "space"), None),
        P(("tm", "space"), None),
        P(("tm", "space"), None),
        P("tm", None, None),
        P(),
        P(),
        P(),
    )
    out_specs = (P("tm", "space", None, None, None), P(("tm", "space"), None))
    return jax.shard_map(shards, mesh=mesh, in_specs=in_specs, out_specs=out_specs, check_vma=False)
```

```python
import functools
import math

import jax
import jax.numpy as jnp
from jax import lax
from jax.experimental import pallas as pl
from jax.experimental.pallas import tpu as pltpu
from jax.sharding import PartitionSpec as P

HD = 128
TF = 6
TC = 8
TILE = 384
CELL = 2 * TILE
PIECE = TF * TC
GW = 384
GH = GW // HD
TXT = 256
EXTRA = 16
COLUMNS = 512
AXES = ("tm", "space")
SCALE = HD**-0.5 * math.log2(math.e)
MASKED = -1e30
TEXT_LANE = 4
CONTRACT_LAST = (((1,), (1,)), ((), ()))


def device(y, z, x, c):
    return (2 * y + z % 2) * 16 + 8 * (z // 2) + 2 * x + c


PLACES = [(y, z, x, c) for y in range(4) for z in range(4) for x in range(4) for c in range(2)]
PLANES = [
    [device(y, z, x, c) for z in range(4) for x in range(4)] for y in range(4) for c in range(2)
]


SAME_PLACE = [
    [device(y, z, x, c) for y in range(4) for c in range(2)] for z in range(4) for x in range(4)
]


def route(target):
    pairs = []
    for place in PLACES:
        goal = target(*place)
        if goal is not None:
            pairs.append((device(*place), device(*goal)))
    return pairs


def in_time(steps):
    def target(y, z, x, c):
        moment = 2 * y + c + steps
        return (moment // 2, z, x, moment % 2) if 0 <= moment < 8 else None

    return route(target)


def in_columns(steps):
    return route(lambda y, z, x, c: (y, z, x + steps, c) if 0 <= x + steps < 4 else None)


def to_owner(turn):
    def target(y, z, x, c):
        tile = (z + turn) % 4
        return (y, 2 * (x // 2) + c, 2 * (x % 2) + tile // 2, tile % 2)

    return route(target)


OTHER_CORE = route(lambda y, z, x, c: (y, z, x, 1 - c))


TIME_PARTNER = route(lambda y, z, x, c: (y, z ^ 1, x, c))


def send(value, pairs):
    return lax.ppermute(value, AXES, pairs)


def exchange(value, groups):
    return lax.all_to_all(
        value, AXES, split_axis=0, concat_axis=0, tiled=True, axis_index_groups=groups
    )


def pack_kernel(k_ref, v_ref, out_ref):
    for p in range(4):
        columns = slice(2 * TC * p, 2 * TC * (p + 1))
        for kind, ref in enumerate((k_ref, v_ref)):
            cut = ref[:, columns, :].astype(jnp.float32).reshape(TF, 2, TC, GW)
            for w in range(2):
                piece = cut[:, w].reshape(PIECE, GW).astype(jnp.bfloat16)
                out_ref[p, (2 * w + kind) * PIECE : (2 * w + kind + 1) * PIECE] = piece


def pack_queries_kernel(q_ref, text_ref, out_ref):
    for p in range(4):
        rows = q_ref[:, 2 * TC * p : 2 * TC * (p + 1), :].reshape(2 * PIECE, GW)
        out_ref[p, : 2 * PIECE] = rows
        out_ref[p, 2 * PIECE :] = text_ref[...]


def pack(kernel, rows, rasters, *text):
    raster = pl.BlockSpec((TF, 8 * TC, GW), lambda g: (0, 0, g))
    text_spec = pl.BlockSpec((PIECE, GW), lambda g: (0, g))
    return pl.pallas_call(
        kernel,
        grid=(4,),
        in_specs=[raster] * len(rasters) + [text_spec] * len(text),
        out_specs=pl.BlockSpec((4, rows, GW), lambda g: (g, 0, 0)),
        out_shape=jax.ShapeDtypeStruct((16, rows, GW), jnp.bfloat16),
        compiler_params=pltpu.CompilerParams(vmem_limit_bytes=56 * 2**20),
        cost_estimate=pl.CostEstimate(flops=0, bytes_accessed=16 * rows * GW * 4, transcendentals=0),
        name="pack",
    )(*[array.reshape(TF, 8 * TC, 4 * GW) for array in rasters], *text)


def merge_sides_kernel(c_ref, mine_ref, other_ref, low_ref, high_ref):
    for x in range(4):
        for part, get in enumerate((lambda s: mine_ref[0, 0, x, s], lambda s: other_ref[0, x, s])):
            for w, ref in enumerate((low_ref, high_ref)):
                for kind in range(2):
                    start = (2 * x + part) * PIECE
                    rows = slice((2 * w + kind) * PIECE, (2 * w + kind + 1) * PIECE)
                    ref[kind, start : start + PIECE] = get(rows)


def merge_kernel(c_ref, mine_ref, other_ref, own_ref):
    for x in range(4):
        for part, get in enumerate((lambda s: mine_ref[0, 0, x, s], lambda s: other_ref[0, x, s])):
            for w in range(2):
                for kind in range(2):
                    start = (2 * x + part) * PIECE
                    rows = slice((2 * w + kind) * PIECE, (2 * w + kind + 1) * PIECE)
                    own_ref[kind, w, start : start + PIECE] = get(rows)


def merge_queries_kernel(c_ref, mine_ref, other_ref, q_ref):
    even_core = c_ref[0] == 0
    for x in range(4):
        for f in range(TF):
            rows = slice(2 * TC * f, 2 * TC * (f + 1))
            mine = mine_ref[0, 0, x, rows].astype(jnp.float32)
            other = other_ref[0, x, rows].astype(jnp.float32)
            even = jnp.where(even_core, mine, other)
            odd = jnp.where(even_core, other, mine)
            start = (4 * f + x) * 2 * TC
            for w in range(2):
                both = [part[w * TC : (w + 1) * TC] for part in (even, odd)]
                q_ref[w, 0, start : start + 2 * TC] = jnp.concatenate(both).astype(jnp.bfloat16)


def from_other_core(core, got):
    rows = got.shape[1]
    pieces = got.reshape(2, 2, 4, rows, GW)
    other = send(lax.dynamic_index_in_dim(pieces, 1 - core[0], 1, keepdims=False), OTHER_CORE)
    return pieces, other


def merge(core, pieces, other, kernel, out_specs, out_shape):
    rows = pieces.shape[3]
    return pl.pallas_call(
        kernel,
        grid_spec=pltpu.PrefetchScalarGridSpec(
            num_scalar_prefetch=1,
            grid=(2,),
            in_specs=[
                pl.BlockSpec((1, 1, 4, rows, GW), lambda b, c: (b, c[0], 0, 0, 0)),
                pl.BlockSpec((1, 4, rows, GW), lambda b, c: (b, 0, 0, 0)),
            ],
            out_specs=out_specs,
        ),
        out_shape=out_shape,
        compiler_params=pltpu.CompilerParams(vmem_limit_bytes=56 * 2**20),
        cost_estimate=pl.CostEstimate(flops=0, bytes_accessed=16 * rows * GW * 4, transcendentals=0),
        name="merge",
    )(core, pieces, other)


def merge_sides(core, pieces, other):
    cell = pl.BlockSpec((2, TILE, GW), lambda b, c: (0, b, 0))
    shape = jax.ShapeDtypeStruct((2, CELL, GW), jnp.bfloat16)
    return merge(core, pieces, other, merge_sides_kernel, [cell, cell], [shape, shape])


def merge_keys(core, pieces, other):
    both = pl.BlockSpec((2, 2, TILE, GW), lambda b, c: (0, 0, b, 0))
    shape = jax.ShapeDtypeStruct((2, 2, CELL, GW), jnp.bfloat16)
    return merge(core, pieces, other, merge_kernel, both, shape)


def merge_queries(core, pieces, other):
    spec = pl.BlockSpec((2, 1, TILE, GW), lambda b, c: (0, b, 0, 0))
    shape = jax.ShapeDtypeStruct((2, 2, TILE, GW), jnp.bfloat16)
    return merge(core, pieces, other, merge_queries_kernel, spec, shape)


def join_kernel(left_ref, right_ref, out_ref):
    out_ref[:, 0] = left_ref[...]
    out_ref[:, 1] = right_ref[...]


def join(left, right):
    half = pl.BlockSpec((1, CELL, GW), lambda k: (k, 0, 0))
    return pl.pallas_call(
        join_kernel,
        grid=(2,),
        in_specs=[half, half],
        out_specs=pl.BlockSpec((1, 2, CELL, GW), lambda k: (k, 0, 0, 0)),
        out_shape=jax.ShapeDtypeStruct((2, 2, CELL, GW), jnp.bfloat16),
        compiler_params=pltpu.CompilerParams(vmem_limit_bytes=56 * 2**20),
        cost_estimate=pl.CostEstimate(flops=0, bytes_accessed=16 * CELL * GW, transcendentals=0),
        name="join",
    )(left, right)


def project_kernel(from_ref, first, second, third, fourth, weight_ref, out_ref, whole_ref):
    @pl.when(pl.program_id(0) == 0)
    def _():
        for i, ref in enumerate((first, second, third, fourth)):
            whole_ref[:, pl.ds(pl.multiple_of(from_ref[i] * GW, GW), GW)] = ref[...]

    columns = pl.ds(pl.multiple_of(pl.program_id(0) * COLUMNS, COLUMNS), COLUMNS)
    out_ref[...] = jnp.dot(
        whole_ref[...], weight_ref[:, columns], preferred_element_type=jnp.float32
    ).astype(jnp.bfloat16)


def project(groups, parts, weight):
    depth, width = weight.shape
    part = pl.BlockSpec((TILE, GW), lambda n, groups: (0, 0))
    return pl.pallas_call(
        project_kernel,
        grid_spec=pltpu.PrefetchScalarGridSpec(
            num_scalar_prefetch=1,
            grid=(width // COLUMNS,),
            in_specs=[part] * 4 + [pl.BlockSpec(memory_space=pltpu.VMEM)],
            out_specs=pl.BlockSpec((TILE, COLUMNS), lambda n, groups: (0, n)),
            scratch_shapes=[pltpu.VMEM((TILE, depth), jnp.bfloat16)],
        ),
        out_shape=jax.ShapeDtypeStruct((TILE, width), jnp.bfloat16),
        compiler_params=pltpu.CompilerParams(vmem_limit_bytes=24 * 2**20),
        cost_estimate=pl.CostEstimate(
            flops=2 * TILE * depth * width, bytes_accessed=2 * depth * width, transcendentals=0
        ),
        name="project",
    )(groups, *parts, weight)


def wide_bias(table):
    halves = [
        jnp.broadcast_to(table[b][None], (TILE // EXTRA, EXTRA, HD)).reshape(TILE, HD)
        for b in range(2)
    ]
    return jnp.concatenate(halves)


def add_keys(query, state, keys, bias, values):
    ones = jnp.ones((keys.shape[0], HD), jnp.bfloat16)
    scores = lax.dot_general(
        query,
        jnp.concatenate([keys, bias], axis=1),
        CONTRACT_LAST,
        preferred_element_type=jnp.float32,
    )
    top = jnp.max(scores, axis=1, keepdims=True)
    if state is not None:
        top = jnp.maximum(top, state[0])
    weights = jnp.exp2((scores - top) * SCALE).astype(jnp.bfloat16)
    part = jnp.dot(
        weights, jnp.concatenate([values, ones], axis=1), preferred_element_type=jnp.float32
    )
    if state is not None:
        part = part + state[1] * jnp.exp2((state[0] - top) * SCALE)
    return top, part


def widened(query, first_lane):
    rows = query.shape[0]
    lanes = lax.broadcasted_iota(jnp.int32, (rows, HD), 1)
    which = lax.broadcasted_iota(jnp.int32, (rows, HD), 0) // TILE
    hot = jnp.where(lanes == first_lane + which, 1.0, 0.0).astype(jnp.bfloat16)
    return jnp.concatenate([query, hot], axis=1)


def mark_of(state):
    rows = state[1].shape[0]
    lanes = lax.broadcasted_iota(jnp.int32, (rows, HD), 1)
    return jnp.where(lanes < HD // 2, jnp.broadcast_to(state[0], (rows, HD)), state[1][:, HD:])


def near_kernel(cells, q_ref, tk_ref, tv_ref, bias_ref, *refs):
    sum_ref, mark_ref = refs[2 * cells :]
    no_bias = jnp.zeros((TXT, HD), jnp.bfloat16)
    for w in range(2):
        query = widened(q_ref[w].reshape(CELL, HD), 2 * w)
        state = add_keys(query, None, tk_ref[0], no_bias, tv_ref[0])
        for i in range(2 * cells):
            bias = wide_bias(bias_ref[i])
            keys, values = refs[2 * (i // 2)], refs[2 * (i // 2) + 1]
            state = add_keys(query, state, keys[0, i % 2], bias, values[0, i % 2])
        sum_ref[w] = state[1][:, :HD]
        mark_ref[w] = mark_of(state)


def cell_specs(number):
    def spec(kind):
        return pl.BlockSpec((1, 2, CELL, HD), lambda h: (kind, 0, 0, h))

    return [spec(0), spec(1)] * number


def doubled(cells):
    return [array for cell in cells for array in (cell, cell)]


def cost(rows, keys, heads):
    return pl.CostEstimate(
        flops=rows * keys * heads * 4 * 384,
        bytes_accessed=4 * keys * heads * HD,
        transcendentals=rows * keys * heads,
    )


def near(queries, text_all, bias, cells):
    state = pl.BlockSpec((2, CELL, HD), lambda h: (0, 0, h))
    shape = jax.ShapeDtypeStruct((2, CELL, GW), jnp.float32)
    return pl.pallas_call(
        functools.partial(near_kernel, len(cells)),
        grid=(GH,),
        in_specs=[
            pl.BlockSpec((2, 2, TILE, HD), lambda h: (0, 0, 0, h)),
            pl.BlockSpec((1, TXT, HD), lambda h: (1, 0, h)),
            pl.BlockSpec((1, TXT, HD), lambda h: (2, 0, h)),
            pl.BlockSpec(bias.shape, lambda h: (0, 0, 0, 0)),
        ]
        + cell_specs(len(cells)),
        out_specs=[state, state],
        out_shape=[shape, shape],
        compiler_params=pltpu.CompilerParams(vmem_limit_bytes=40 * 2**20),
        cost_estimate=cost(2 * CELL, 2 * len(cells) * CELL + TXT, GH),
        name="near_cells",
    )(queries, text_all, text_all, bias, *doubled(cells))


def side_kernel(valid_ref, q_ref, sum_ref, mark_ref, bias_ref, *refs):
    out_ref = refs[6]
    row = lax.broadcasted_iota(jnp.int32, (CELL, HD), 0)
    for w in range(2):
        query = widened(q_ref[w].reshape(CELL, HD), 2 * w)
        mark = mark_ref[w]
        totals = jnp.broadcast_to(mark[:, HD // 2 : HD // 2 + 1], (CELL, HD))
        state = (mark[:, :1], jnp.concatenate([sum_ref[w], totals], axis=1))
        for i in range(3):
            bias = wide_bias(bias_ref[3 * w + i])
            state = add_keys(query, state, refs[2 * i][0, w], bias, refs[2 * i + 1][0, w])
        value = state[1][:, :HD] / state[1][:, HD:]
        value = jnp.where(row % TC < valid_ref[w], value, 0.0).astype(jnp.bfloat16)
        out_ref[w] = value.reshape(2, TILE, HD)


def side(valid, queries, state, bias, cells):
    tall = pl.BlockSpec((2, CELL, HD), lambda h: (0, 0, h))
    query = pl.BlockSpec((2, 2, TILE, HD), lambda h: (0, 0, 0, h))
    return pl.pallas_call(
        side_kernel,
        grid=(GH,),
        in_specs=[
            pl.BlockSpec(memory_space=pltpu.SMEM),
            query,
            tall,
            tall,
            pl.BlockSpec(bias.shape, lambda h: (0, 0, 0, 0)),
        ]
        + cell_specs(3),
        out_specs=query,
        out_shape=jax.ShapeDtypeStruct((2, 2, TILE, GW), jnp.bfloat16),
        compiler_params=pltpu.CompilerParams(vmem_limit_bytes=40 * 2**20),
        cost_estimate=cost(2 * CELL, 3 * CELL, GH),
        name="side_cells",
    )(valid, queries, *state, bias, *doubled(cells))


def text_kernel(share_ref, q_ref, tk_ref, tv_ref, bias_ref, *refs):
    out_ref = refs[2]
    head = pl.program_id(0)
    lanes = lax.broadcasted_iota(jnp.int32, (TXT, HD), 1)
    rows = lax.broadcasted_iota(jnp.int32, (TXT, HD), 0)
    hot = jnp.where(lanes == TEXT_LANE, 1.0, 0.0).astype(jnp.bfloat16)
    query = jnp.concatenate([q_ref[0], hot], axis=1)
    share = jnp.where(rows // 8 == share_ref[0], 0.0, MASKED).astype(jnp.bfloat16)
    state = None
    for i in range(2):
        bias = wide_bias(bias_ref[i])
        state = add_keys(query, state, refs[0][0, i], bias, refs[1][0, i])
    state = add_keys(query, state, tk_ref[0], share, tv_ref[0])
    out_ref[:, pl.ds(pl.multiple_of(head * HD, HD), HD)] = state[1][:, :HD]
    mark = jnp.where(
        lanes % 8 == head, jnp.where(lanes < 8, state[0], state[1][:, HD:]), 0.0
    )

    @pl.when(head == 0)
    def _():
        out_ref[:, GW:] = mark

    @pl.when(head > 0)
    def _():
        out_ref[:, GW:] += mark


def text_part(share, text_all, bias, cells):
    def spec(kind):
        return pl.BlockSpec((1, TXT, HD), lambda h: (kind, 0, h))

    return pl.pallas_call(
        text_kernel,
        grid=(GH,),
        in_specs=[
            pl.BlockSpec(memory_space=pltpu.SMEM),
            spec(0),
            spec(1),
            spec(2),
            pl.BlockSpec(bias.shape, lambda h: (0, 0, 0, 0)),
        ]
        + cell_specs(1),
        out_specs=pl.BlockSpec((TXT, GW + HD), lambda h: (0, 0)),
        out_shape=jax.ShapeDtypeStruct((TXT, GW + HD), jnp.float32),
        compiler_params=pltpu.CompilerParams(vmem_limit_bytes=56 * 2**20),
        cost_estimate=cost(TXT, 2 * CELL + TXT, GH),
        name="text_queries",
    )(share, text_all, text_all, text_all, bias, *doubled(cells))


def text_sum_kernel(part_ref, out_ref):
    for z in range(4):
        marks = part_ref[:, z % 2, z // 2, :, :, GW:]
        top = jnp.max(marks, axis=(0, 1), keepdims=True)
        factors = jnp.exp2((marks - top) * SCALE)
        for h in range(GH):
            factor = factors[..., h : h + 1]
            total = jnp.sum(marks[..., 8 + h : 9 + h] * factor, axis=(0, 1))
            part = part_ref[:, z % 2, z // 2, :, :, h * HD : (h + 1) * HD]
            summed = jnp.sum(part * factor, axis=(0, 1)) / total
            start = z * GW + h * HD
            out_ref[:, start : start + HD] = summed.astype(jnp.bfloat16)


def text_sum(parts):
    return pl.pallas_call(
        text_sum_kernel,
        out_shape=jax.ShapeDtypeStruct((2, 4 * GW), jnp.bfloat16),
        compiler_params=pltpu.CompilerParams(vmem_limit_bytes=56 * 2**20),
        cost_estimate=pl.CostEstimate(
            flops=0, bytes_accessed=TXT * (GW + HD) * 4, transcendentals=0
        ),
        name="text_sum",
    )(parts.reshape(4, 2, 2, 8, 2, GW + HD))


def shards(
    video_query,
    video_key,
    video_value,
    text_query,
    text_key,
    text_value,
    window_lists,
    valid_columns,
    video_weight,
    text_weight,
):
    tm, space = lax.axis_index("tm"), lax.axis_index("space")
    y, zl = tm // 2, tm % 2
    zh, x, c = space // 8, space // 2 % 4, space % 2
    z = 2 * zh + zl
    moment = 2 * y + c

    packed = pack(pack_kernel, 4 * PIECE, [video_key, video_value])
    packed, lists = lax.optimization_barrier((packed, window_lists))
    got = exchange(packed, PLANES)

    other_lists = send(lists, TIME_PARTNER)
    text_rows = jnp.concatenate([text_query, text_key, text_value], axis=0)
    text_some = lax.all_gather(text_rows, AXES, axis_index_groups=SAME_PLACE, tiled=True)
    packed_queries = pack(pack_queries_kernel, 3 * PIECE, [video_query], text_some)
    got, packed_queries = lax.optimization_barrier((got, packed_queries))

    core = c.reshape(1)
    pieces, other = from_other_core(core, got)
    low, high = merge_sides(core, pieces, other)

    left, right = send(high, in_columns(1)), send(low, in_columns(-1))
    other, _ = lax.optimization_barrier((other, low))
    own = merge_keys(core, pieces, other)
    past, future = send(own, in_time(1)), send(own, in_time(-1))
    packed_queries, _ = lax.optimization_barrier((packed_queries, own))
    got_queries = exchange(packed_queries, PLANES)
    queries = merge_queries(core, *from_other_core(core, got_queries))

    text_all = got_queries[:, 2 * PIECE :].reshape(2, 2, 4, 4, 2, 3, 2, GW)
    text_all = text_all.transpose(5, 3, 1, 0, 2, 4, 6, 7).reshape(3, TXT, GW)

    got_lists = jnp.where(zl == c, lists, other_lists).reshape(2, 8, 27)
    tile_lists = lax.dynamic_slice_in_dim(got_lists, 2 * x, 2, 1).transpose(1, 0, 2).reshape(4, 27)
    key_moment = moment + jnp.arange(-1, 2, dtype=jnp.int32)[:, None, None]
    key_column = 2 * x + jnp.arange(-1, 3, dtype=jnp.int32)[None, :, None]
    key_band = jnp.arange(2, dtype=jnp.int32)[None, None, :]
    inside = (key_moment >= 0) & (key_moment < 8) & (key_column >= 0) & (key_column < 8)
    idents = jnp.where(inside, 16 * key_moment + 8 * key_band + key_column, -2)
    listed = jnp.any(idents[..., None, None] == tile_lists, axis=-1)
    places = jnp.arange(8, dtype=jnp.int32)
    columns = 2 * x + jnp.arange(-1, 3, dtype=jnp.int32)
    valid = jnp.sum(
        jnp.where(places[None, :] == columns[:, None], valid_columns[None, :], 0), axis=1
    )
    fine = (jnp.arange(EXTRA, dtype=jnp.int32) % TC)[None, :] < valid[:, None]
    listed = jnp.pad(listed, ((0, 0), (0, 0), (0, 0), (0, HD - 4)), constant_values=True)
    allowed = listed[:, :, :, None, :] & fine[None, :, None, :, None]
    bias = jnp.where(allowed, 0.0, MASKED).astype(jnp.bfloat16)
    near_bias = jnp.concatenate([bias[1, 1:3], bias[0, 1:3], bias[2, 1:3]])
    side_bias = jnp.concatenate([bias[:, 0], bias[:, 3]])

    member = (4 * y + x) * 2 + c
    parts = text_part(member.reshape(1), text_all, near_bias[:2], [own])
    left, right, _, queries = lax.optimization_barrier((left, right, parts, queries))
    parts = exchange(parts.reshape(128, 2, GW + HD), None)
    sides = join(left, right)
    past_sides, future_sides = send(sides, in_time(1)), send(sides, in_time(-1))

    state = near(queries, text_all, near_bias, [own, past, future])
    attended = side(valid[1:3], queries, state, side_bias, [past_sides, sides, future_sides])
    parts, attended = lax.optimization_barrier((parts, attended))
    attended = attended.reshape(4, TILE, GW)

    turns = jnp.arange(4, dtype=jnp.int32)
    arrived = [
        send(lax.dynamic_index_in_dim(attended, (z + turn) % 4, 0, keepdims=False), to_owner(turn))
        for turn in range(4)
    ]
    video_output = project((2 * (x % 2) + c - turns) % 4, arrived, video_weight)
    video_output = video_output.reshape(1, 1, 1, TILE, -1)
    text_attn = text_sum(parts)
    text_output = jnp.dot(text_attn, text_weight, preferred_element_type=jnp.float32)
    text_output = text_output.astype(jnp.bfloat16)
    return (video_output, text_output)


def solution(mesh):
    in_specs = (
        P("tm", "space", None, None),
        P("tm", "space", None, None),
        P("tm", "space", None, None),
        P(("tm", "space"), None),
        P(("tm", "space"), None),
        P(("tm", "space"), None),
        P("tm", None, None),
        P(),
        P(),
        P(),
    )
    out_specs = (P("tm", "space", None, None, None), P(("tm", "space"), None))
    return jax.shard_map(shards, mesh=mesh, in_specs=in_specs, out_specs=out_specs, check_vma=False)
```

```python
import functools
import math

import jax
import jax.numpy as jnp
from jax import lax
from jax.experimental import pallas as pl
from jax.experimental.pallas import tpu as pltpu
from jax.sharding import PartitionSpec as P

HD = 128
TF = 6
TC = 8
TILE = 384
CELL = 2 * TILE
PIECE = TF * TC
GW = 384
GH = GW // HD
TXT = 256
EXTRA = 16
COLUMNS = 512
AXES = ("tm", "space")
SCALE = HD**-0.5 * math.log2(math.e)
MASKED = -1e30
TOO_FAR = 60.0 / SCALE
TEXT_LANE = 4
CONTRACT_LAST = (((1,), (1,)), ((), ()))


def device(y, z, x, c):
    return (2 * y + z % 2) * 16 + 8 * (z // 2) + 2 * x + c


PLACES = [(y, z, x, c) for y in range(4) for z in range(4) for x in range(4) for c in range(2)]
PLANES = [
    [device(y, z, x, c) for z in range(4) for x in range(4)] for y in range(4) for c in range(2)
]


SAME_PLACE = [
    [device(y, z, x, c) for y in range(4) for c in range(2)] for z in range(4) for x in range(4)
]


def route(target):
    pairs = []
    for place in PLACES:
        goal = target(*place)
        if goal is not None:
            pairs.append((device(*place), device(*goal)))
    return pairs


def in_time(steps):
    def target(y, z, x, c):
        moment = 2 * y + c + steps
        return (moment // 2, z, x, moment % 2) if 0 <= moment < 8 else None

    return route(target)


def in_columns(steps):
    return route(lambda y, z, x, c: (y, z, x + steps, c) if 0 <= x + steps < 4 else None)


def to_owner(turn):
    def target(y, z, x, c):
        tile = (z + turn) % 4
        return (y, 2 * (x // 2) + c, 2 * (x % 2) + tile // 2, tile % 2)

    return route(target)


OTHER_CORE = route(lambda y, z, x, c: (y, z, x, 1 - c))


TIME_PARTNER = route(lambda y, z, x, c: (y, z ^ 1, x, c))


def send(value, pairs):
    return lax.ppermute(value, AXES, pairs)


def exchange(value, groups):
    return lax.all_to_all(
        value, AXES, split_axis=0, concat_axis=0, tiled=True, axis_index_groups=groups
    )


def pack_kernel(k_ref, v_ref, out_ref):
    for p in range(4):
        columns = slice(2 * TC * p, 2 * TC * (p + 1))
        for kind, ref in enumerate((k_ref, v_ref)):
            cut = ref[:, columns, :].astype(jnp.float32).reshape(TF, 2, TC, GW)
            for w in range(2):
                piece = cut[:, w].reshape(PIECE, GW).astype(jnp.bfloat16)
                out_ref[p, (2 * w + kind) * PIECE : (2 * w + kind + 1) * PIECE] = piece


def pack_queries_kernel(q_ref, text_ref, out_ref):
    for p in range(4):
        rows = q_ref[:, 2 * TC * p : 2 * TC * (p + 1), :].reshape(2 * PIECE, GW)
        out_ref[p, : 2 * PIECE] = rows
        out_ref[p, 2 * PIECE :] = text_ref[...]


def pack(kernel, rows, rasters, *text):
    raster = pl.BlockSpec((TF, 8 * TC, GW), lambda g: (0, 0, g))
    text_spec = pl.BlockSpec((PIECE, GW), lambda g: (0, g))
    return pl.pallas_call(
        kernel,
        grid=(4,),
        in_specs=[raster] * len(rasters) + [text_spec] * len(text),
        out_specs=pl.BlockSpec((4, rows, GW), lambda g: (g, 0, 0)),
        out_shape=jax.ShapeDtypeStruct((16, rows, GW), jnp.bfloat16),
        compiler_params=pltpu.CompilerParams(vmem_limit_bytes=56 * 2**20),
        cost_estimate=pl.CostEstimate(flops=0, bytes_accessed=16 * rows * GW * 4, transcendentals=0),
        name="pack",
    )(*[array.reshape(TF, 8 * TC, 4 * GW) for array in rasters], *text)


def merge_sides_kernel(c_ref, mine_ref, other_ref, low_ref, high_ref):
    for x in range(4):
        for part, get in enumerate((lambda s: mine_ref[0, 0, x, s], lambda s: other_ref[0, x, s])):
            for w, ref in enumerate((low_ref, high_ref)):
                for kind in range(2):
                    start = (2 * x + part) * PIECE
                    rows = slice((2 * w + kind) * PIECE, (2 * w + kind + 1) * PIECE)
                    ref[kind, start : start + PIECE] = get(rows)


def merge_kernel(c_ref, mine_ref, other_ref, own_ref):
    for x in range(4):
        for part, get in enumerate((lambda s: mine_ref[0, 0, x, s], lambda s: other_ref[0, x, s])):
            for w in range(2):
                for kind in range(2):
                    start = (2 * x + part) * PIECE
                    rows = slice((2 * w + kind) * PIECE, (2 * w + kind + 1) * PIECE)
                    own_ref[kind, w, start : start + PIECE] = get(rows)


def merge_queries_kernel(c_ref, mine_ref, other_ref, q_ref):
    even_core = c_ref[0] == 0
    for x in range(4):
        for f in range(TF):
            rows = slice(2 * TC * f, 2 * TC * (f + 1))
            mine = mine_ref[0, 0, x, rows].astype(jnp.float32)
            other = other_ref[0, x, rows].astype(jnp.float32)
            even = jnp.where(even_core, mine, other)
            odd = jnp.where(even_core, other, mine)
            start = (4 * f + x) * 2 * TC
            for w in range(2):
                both = [part[w * TC : (w + 1) * TC] for part in (even, odd)]
                q_ref[w, 0, start : start + 2 * TC] = jnp.concatenate(both).astype(jnp.bfloat16)


def from_other_core(core, got):
    rows = got.shape[1]
    pieces = got.reshape(2, 2, 4, rows, GW)
    other = send(lax.dynamic_index_in_dim(pieces, 1 - core[0], 1, keepdims=False), OTHER_CORE)
    return pieces, other


def merge(core, pieces, other, kernel, out_specs, out_shape):
    rows = pieces.shape[3]
    return pl.pallas_call(
        kernel,
        grid_spec=pltpu.PrefetchScalarGridSpec(
            num_scalar_prefetch=1,
            grid=(2,),
            in_specs=[
                pl.BlockSpec((1, 1, 4, rows, GW), lambda b, c: (b, c[0], 0, 0, 0)),
                pl.BlockSpec((1, 4, rows, GW), lambda b, c: (b, 0, 0, 0)),
            ],
            out_specs=out_specs,
        ),
        out_shape=out_shape,
        compiler_params=pltpu.CompilerParams(vmem_limit_bytes=56 * 2**20),
        cost_estimate=pl.CostEstimate(flops=0, bytes_accessed=16 * rows * GW * 4, transcendentals=0),
        name="merge",
    )(core, pieces, other)


def merge_sides(core, pieces, other):
    cell = pl.BlockSpec((2, TILE, GW), lambda b, c: (0, b, 0))
    shape = jax.ShapeDtypeStruct((2, CELL, GW), jnp.bfloat16)
    return merge(core, pieces, other, merge_sides_kernel, [cell, cell], [shape, shape])


def merge_keys(core, pieces, other):
    both = pl.BlockSpec((2, 2, TILE, GW), lambda b, c: (0, 0, b, 0))
    shape = jax.ShapeDtypeStruct((2, 2, CELL, GW), jnp.bfloat16)
    return merge(core, pieces, other, merge_kernel, both, shape)


def merge_queries(core, pieces, other):
    spec = pl.BlockSpec((2, 1, TILE, GW), lambda b, c: (0, b, 0, 0))
    shape = jax.ShapeDtypeStruct((2, 2, TILE, GW), jnp.bfloat16)
    return merge(core, pieces, other, merge_queries_kernel, spec, shape)


def join_kernel(left_ref, right_ref, out_ref):
    out_ref[:, 0] = left_ref[...]
    out_ref[:, 1] = right_ref[...]


def join(left, right):
    half = pl.BlockSpec((1, CELL, GW), lambda k: (k, 0, 0))
    return pl.pallas_call(
        join_kernel,
        grid=(2,),
        in_specs=[half, half],
        out_specs=pl.BlockSpec((1, 2, CELL, GW), lambda k: (k, 0, 0, 0)),
        out_shape=jax.ShapeDtypeStruct((2, 2, CELL, GW), jnp.bfloat16),
        compiler_params=pltpu.CompilerParams(vmem_limit_bytes=56 * 2**20),
        cost_estimate=pl.CostEstimate(flops=0, bytes_accessed=16 * CELL * GW, transcendentals=0),
        name="join",
    )(left, right)


def project_kernel(from_ref, first, second, third, fourth, weight_ref, out_ref, whole_ref):
    @pl.when(pl.program_id(0) == 0)
    def _():
        for i, ref in enumerate((first, second, third, fourth)):
            whole_ref[:, pl.ds(pl.multiple_of(from_ref[i] * GW, GW), GW)] = ref[...]

    columns = pl.ds(pl.multiple_of(pl.program_id(0) * COLUMNS, COLUMNS), COLUMNS)
    out_ref[...] = jnp.dot(
        whole_ref[...], weight_ref[:, columns], preferred_element_type=jnp.float32
    ).astype(jnp.bfloat16)


def project(groups, parts, weight):
    depth, width = weight.shape
    part = pl.BlockSpec((TILE, GW), lambda n, groups: (0, 0))
    return pl.pallas_call(
        project_kernel,
        grid_spec=pltpu.PrefetchScalarGridSpec(
            num_scalar_prefetch=1,
            grid=(width // COLUMNS,),
            in_specs=[part] * 4 + [pl.BlockSpec(memory_space=pltpu.VMEM)],
            out_specs=pl.BlockSpec((TILE, COLUMNS), lambda n, groups: (0, n)),
            scratch_shapes=[pltpu.VMEM((TILE, depth), jnp.bfloat16)],
        ),
        out_shape=jax.ShapeDtypeStruct((TILE, width), jnp.bfloat16),
        compiler_params=pltpu.CompilerParams(vmem_limit_bytes=24 * 2**20),
        cost_estimate=pl.CostEstimate(
            flops=2 * TILE * depth * width, bytes_accessed=2 * depth * width, transcendentals=0
        ),
        name="project",
    )(groups, *parts, weight)


def wide_bias(table):
    halves = [
        jnp.broadcast_to(table[b][None], (TILE // EXTRA, EXTRA, HD)).reshape(TILE, HD)
        for b in range(2)
    ]
    return jnp.concatenate(halves)


def add_keys(query, state, keys, bias, values):
    ones = jnp.ones((keys.shape[0], HD), jnp.bfloat16)
    scores = lax.dot_general(
        query,
        jnp.concatenate([keys, bias], axis=1),
        CONTRACT_LAST,
        preferred_element_type=jnp.float32,
    )
    top = jnp.max(scores, axis=1, keepdims=True)
    if state is not None:
        top = jnp.maximum(top, state[0])
    weights = jnp.exp2((scores - top) * SCALE).astype(jnp.bfloat16)
    part = jnp.dot(
        weights, jnp.concatenate([values, ones], axis=1), preferred_element_type=jnp.float32
    )
    if state is not None:
        part = part + state[1] * jnp.exp2((state[0] - top) * SCALE)
    return top, part


def add_all(query, state, blocks):
    for keys, bias, values in blocks:
        state = add_keys(query, state, keys(), wide_bias(bias()), values())
    return state, None


def add_all_late(query, state, blocks):
    peak, total = state
    step = None
    for keys, bias, values in blocks:
        scores = lax.dot_general(
            query,
            jnp.concatenate([keys(), wide_bias(bias())], axis=1),
            CONTRACT_LAST,
            preferred_element_type=jnp.float32,
        )
        weights = jnp.exp2((scores - peak) * SCALE).astype(jnp.bfloat16)
        ones = jnp.ones((CELL, HD), jnp.bfloat16)
        part = jnp.dot(
            weights, jnp.concatenate([values(), ones], axis=1), preferred_element_type=jnp.float32
        )
        top = jnp.maximum(peak, jnp.max(scores, axis=1, keepdims=True))
        rise = top - peak
        total = (total + part) * jnp.exp2(-rise * SCALE)
        step = rise if step is None else jnp.maximum(step, rise)
        peak = top
    return (peak, total), jnp.max(step)


def widened(query, first_lane):
    rows = query.shape[0]
    lanes = lax.broadcasted_iota(jnp.int32, (rows, HD), 1)
    which = lax.broadcasted_iota(jnp.int32, (rows, HD), 0) // TILE
    hot = jnp.where(lanes == first_lane + which, 1.0, 0.0).astype(jnp.bfloat16)
    return jnp.concatenate([query, hot], axis=1)


def mark_of(state):
    rows = state[1].shape[0]
    lanes = lax.broadcasted_iota(jnp.int32, (rows, HD), 1)
    return jnp.where(lanes < HD // 2, jnp.broadcast_to(state[0], (rows, HD)), state[1][:, HD:])


def near_kernel(cells, q_ref, tk_ref, tv_ref, bias_ref, *refs):
    sum_ref, mark_ref = refs[2 * cells :]

    def run(w, late):
        query = widened(q_ref[w].reshape(CELL, HD), 2 * w)
        no_bias = jnp.zeros((TXT, HD), jnp.bfloat16)
        state = add_keys(query, None, tk_ref[0], no_bias, tv_ref[0])
        blocks = [
            (
                functools.partial(refs[2 * (i // 2)].__getitem__, (0, i % 2)),
                functools.partial(bias_ref.__getitem__, i),
                functools.partial(refs[2 * (i // 2) + 1].__getitem__, (0, i % 2)),
            )
            for i in range(2 * cells)
        ]
        state, _ = late(query, state, blocks)
        sum_ref[w] = state[1][:, :HD]
        mark_ref[w] = mark_of(state)

    run(0, add_all)
    run(1, add_all)


def cell_specs(number):
    def spec(kind):
        return pl.BlockSpec((1, 2, CELL, HD), lambda h: (kind, 0, 0, h))

    return [spec(0), spec(1)] * number


def doubled(cells):
    return [array for cell in cells for array in (cell, cell)]


def cost(rows, keys, heads):
    return pl.CostEstimate(
        flops=rows * keys * heads * 4 * 384,
        bytes_accessed=4 * keys * heads * HD,
        transcendentals=rows * keys * heads,
    )


def near(queries, text_all, bias, cells):
    state = pl.BlockSpec((2, CELL, HD), lambda h: (0, 0, h))
    shape = jax.ShapeDtypeStruct((2, CELL, GW), jnp.float32)
    return pl.pallas_call(
        functools.partial(near_kernel, len(cells)),
        grid=(GH,),
        in_specs=[
            pl.BlockSpec((2, 2, TILE, HD), lambda h: (0, 0, 0, h)),
            pl.BlockSpec((1, TXT, HD), lambda h: (1, 0, h)),
            pl.BlockSpec((1, TXT, HD), lambda h: (2, 0, h)),
            pl.BlockSpec(bias.shape, lambda h: (0, 0, 0, 0)),
        ]
        + cell_specs(len(cells)),
        out_specs=[state, state],
        out_shape=[shape, shape],
        compiler_params=pltpu.CompilerParams(vmem_limit_bytes=40 * 2**20),
        cost_estimate=cost(2 * CELL, 2 * len(cells) * CELL + TXT, GH),
        name="near_cells",
    )(queries, text_all, text_all, bias, *doubled(cells))


def side_kernel(valid_ref, q_ref, sum_ref, mark_ref, bias_ref, *refs):
    out_ref = refs[6]
    row = lax.broadcasted_iota(jnp.int32, (CELL, HD), 0)

    def run(w, late):
        query = widened(q_ref[w].reshape(CELL, HD), 2 * w)
        mark = mark_ref[w]
        totals = jnp.broadcast_to(mark[:, HD // 2 : HD // 2 + 1], (CELL, HD))
        state = (mark[:, :1], jnp.concatenate([sum_ref[w], totals], axis=1))
        blocks = [
            (
                functools.partial(refs[2 * i].__getitem__, (0, w)),
                functools.partial(bias_ref.__getitem__, 3 * w + i),
                functools.partial(refs[2 * i + 1].__getitem__, (0, w)),
            )
            for i in range(3)
        ]
        state, step = late(query, state, blocks)
        value = state[1][:, :HD] / state[1][:, HD:]
        value = jnp.where(row % TC < valid_ref[w], value, 0.0).astype(jnp.bfloat16)
        out_ref[w] = value.reshape(2, TILE, HD)
        return step

    step = jnp.maximum(run(0, add_all_late), run(1, add_all_late))

    @pl.when(step > TOO_FAR)
    def _():
        run(0, add_all)
        run(1, add_all)


def side(valid, queries, state, bias, cells):
    tall = pl.BlockSpec((2, CELL, HD), lambda h: (0, 0, h))
    query = pl.BlockSpec((2, 2, TILE, HD), lambda h: (0, 0, 0, h))
    return pl.pallas_call(
        side_kernel,
        grid=(GH,),
        in_specs=[
            pl.BlockSpec(memory_space=pltpu.SMEM),
            query,
            tall,
            tall,
            pl.BlockSpec(bias.shape, lambda h: (0, 0, 0, 0)),
        ]
        + cell_specs(3),
        out_specs=query,
        out_shape=jax.ShapeDtypeStruct((2, 2, TILE, GW), jnp.bfloat16),
        compiler_params=pltpu.CompilerParams(vmem_limit_bytes=40 * 2**20),
        cost_estimate=cost(2 * CELL, 3 * CELL, GH),
        name="side_cells",
    )(valid, queries, *state, bias, *doubled(cells))


def text_kernel(share_ref, q_ref, tk_ref, tv_ref, bias_ref, *refs):
    out_ref = refs[2]
    head = pl.program_id(0)
    lanes = lax.broadcasted_iota(jnp.int32, (TXT, HD), 1)
    rows = lax.broadcasted_iota(jnp.int32, (TXT, HD), 0)
    hot = jnp.where(lanes == TEXT_LANE, 1.0, 0.0).astype(jnp.bfloat16)
    query = jnp.concatenate([q_ref[0], hot], axis=1)
    share = jnp.where(rows // 8 == share_ref[0], 0.0, MASKED).astype(jnp.bfloat16)
    state = None
    for i in range(2):
        bias = wide_bias(bias_ref[i])
        state = add_keys(query, state, refs[0][0, i], bias, refs[1][0, i])
    state = add_keys(query, state, tk_ref[0], share, tv_ref[0])
    out_ref[:, pl.ds(pl.multiple_of(head * HD, HD), HD)] = state[1][:, :HD]
    mark = jnp.where(
        lanes % 8 == head, jnp.where(lanes < 8, state[0], state[1][:, HD:]), 0.0
    )

    @pl.when(head == 0)
    def _():
        out_ref[:, GW:] = mark

    @pl.when(head > 0)
    def _():
        out_ref[:, GW:] += mark


def text_part(share, text_all, bias, cells):
    def spec(kind):
        return pl.BlockSpec((1, TXT, HD), lambda h: (kind, 0, h))

    return pl.pallas_call(
        text_kernel,
        grid=(GH,),
        in_specs=[
            pl.BlockSpec(memory_space=pltpu.SMEM),
            spec(0),
            spec(1),
            spec(2),
            pl.BlockSpec(bias.shape, lambda h: (0, 0, 0, 0)),
        ]
        + cell_specs(1),
        out_specs=pl.BlockSpec((TXT, GW + HD), lambda h: (0, 0)),
        out_shape=jax.ShapeDtypeStruct((TXT, GW + HD), jnp.float32),
        compiler_params=pltpu.CompilerParams(vmem_limit_bytes=56 * 2**20),
        cost_estimate=cost(TXT, 2 * CELL + TXT, GH),
        name="text_queries",
    )(share, text_all, text_all, text_all, bias, *doubled(cells))


def text_sum_kernel(part_ref, out_ref):
    for z in range(4):
        marks = part_ref[:, z % 2, z // 2, :, :, GW:]
        top = jnp.max(marks, axis=(0, 1), keepdims=True)
        factors = jnp.exp2((marks - top) * SCALE)
        for h in range(GH):
            factor = factors[..., h : h + 1]
            total = jnp.sum(marks[..., 8 + h : 9 + h] * factor, axis=(0, 1))
            part = part_ref[:, z % 2, z // 2, :, :, h * HD : (h + 1) * HD]
            summed = jnp.sum(part * factor, axis=(0, 1)) / total
            start = z * GW + h * HD
            out_ref[:, start : start + HD] = summed.astype(jnp.bfloat16)


def text_sum(parts):
    return pl.pallas_call(
        text_sum_kernel,
        out_shape=jax.ShapeDtypeStruct((2, 4 * GW), jnp.bfloat16),
        compiler_params=pltpu.CompilerParams(vmem_limit_bytes=56 * 2**20),
        cost_estimate=pl.CostEstimate(
            flops=0, bytes_accessed=TXT * (GW + HD) * 4, transcendentals=0
        ),
        name="text_sum",
    )(parts.reshape(4, 2, 2, 8, 2, GW + HD))


def shards(
    video_query,
    video_key,
    video_value,
    text_query,
    text_key,
    text_value,
    window_lists,
    valid_columns,
    video_weight,
    text_weight,
):
    tm, space = lax.axis_index("tm"), lax.axis_index("space")
    y, zl = tm // 2, tm % 2
    zh, x, c = space // 8, space // 2 % 4, space % 2
    z = 2 * zh + zl
    moment = 2 * y + c

    packed = pack(pack_kernel, 4 * PIECE, [video_key, video_value])
    packed, lists = lax.optimization_barrier((packed, window_lists))
    got = exchange(packed, PLANES)

    other_lists = send(lists, TIME_PARTNER)
    text_rows = jnp.concatenate([text_query, text_key, text_value], axis=0)
    text_some = lax.all_gather(text_rows, AXES, axis_index_groups=SAME_PLACE, tiled=True)
    packed_queries = pack(pack_queries_kernel, 3 * PIECE, [video_query], text_some)
    got, packed_queries = lax.optimization_barrier((got, packed_queries))

    core = c.reshape(1)
    pieces, other = from_other_core(core, got)
    low, high = merge_sides(core, pieces, other)

    left, right = send(high, in_columns(1)), send(low, in_columns(-1))
    other, _ = lax.optimization_barrier((other, low))
    own = merge_keys(core, pieces, other)
    past, future = send(own, in_time(1)), send(own, in_time(-1))
    got_queries = exchange(packed_queries, PLANES)
    queries = merge_queries(core, *from_other_core(core, got_queries))

    text_all = got_queries[:, 2 * PIECE :].reshape(2, 2, 4, 4, 2, 3, 2, GW)
    text_all = text_all.transpose(5, 3, 1, 0, 2, 4, 6, 7).reshape(3, TXT, GW)

    got_lists = jnp.where(zl == c, lists, other_lists).reshape(2, 8, 27)
    tile_lists = lax.dynamic_slice_in_dim(got_lists, 2 * x, 2, 1).transpose(1, 0, 2).reshape(4, 27)
    key_moment = moment + jnp.arange(-1, 2, dtype=jnp.int32)[:, None, None]
    key_column = 2 * x + jnp.arange(-1, 3, dtype=jnp.int32)[None, :, None]
    key_band = jnp.arange(2, dtype=jnp.int32)[None, None, :]
    inside = (key_moment >= 0) & (key_moment < 8) & (key_column >= 0) & (key_column < 8)
    idents = jnp.where(inside, 16 * key_moment + 8 * key_band + key_column, -2)
    listed = jnp.any(idents[..., None, None] == tile_lists, axis=-1)
    places = jnp.arange(8, dtype=jnp.int32)
    columns = 2 * x + jnp.arange(-1, 3, dtype=jnp.int32)
    valid = jnp.sum(
        jnp.where(places[None, :] == columns[:, None], valid_columns[None, :], 0), axis=1
    )
    fine = (jnp.arange(EXTRA, dtype=jnp.int32) % TC)[None, :] < valid[:, None]
    listed = jnp.pad(listed, ((0, 0), (0, 0), (0, 0), (0, HD - 4)), constant_values=True)
    allowed = listed[:, :, :, None, :] & fine[None, :, None, :, None]
    bias = jnp.where(allowed, 0.0, MASKED).astype(jnp.bfloat16)
    near_bias = jnp.concatenate([bias[1, 1:3], bias[0, 1:3], bias[2, 1:3]])
    side_bias = jnp.concatenate([bias[:, 0], bias[:, 3]])

    member = (4 * y + x) * 2 + c
    parts = text_part(member.reshape(1), text_all, near_bias[:2], [own])
    left, right, _, queries = lax.optimization_barrier((left, right, parts, queries))
    parts = exchange(parts.reshape(128, 2, GW + HD), None)
    sides = join(left, right)
    past_sides, future_sides = send(sides, in_time(1)), send(sides, in_time(-1))

    state = near(queries, text_all, near_bias, [own, past, future])
    attended = side(valid[1:3], queries, state, side_bias, [past_sides, sides, future_sides])
    parts, attended = lax.optimization_barrier((parts, attended))
    attended = attended.reshape(4, TILE, GW)

    turns = jnp.arange(4, dtype=jnp.int32)
    arrived = [
        send(lax.dynamic_index_in_dim(attended, (z + turn) % 4, 0, keepdims=False), to_owner(turn))
        for turn in range(4)
    ]
    video_output = project((2 * (x % 2) + c - turns) % 4, arrived, video_weight)
    video_output = video_output.reshape(1, 1, 1, TILE, -1)
    text_attn = text_sum(parts)
    text_output = jnp.dot(text_attn, text_weight, preferred_element_type=jnp.float32)
    text_output = text_output.astype(jnp.bfloat16)
    return (video_output, text_output)


def solution(mesh):
    in_specs = (
        P("tm", "space", None, None),
        P("tm", "space", None, None),
        P("tm", "space", None, None),
        P(("tm", "space"), None),
        P(("tm", "space"), None),
        P(("tm", "space"), None),
        P("tm", None, None),
        P(),
        P(),
        P(),
    )
    out_specs = (P("tm", "space", None, None, None), P(("tm", "space"), None))
    return jax.shard_map(shards, mesh=mesh, in_specs=in_specs, out_specs=out_specs, check_vma=False)
```

```python
import functools
import math

import jax
import jax.numpy as jnp
from jax import lax
from jax.experimental import pallas as pl
from jax.experimental.pallas import tpu as pltpu
from jax.sharding import PartitionSpec as P

HD = 128
TF = 6
TC = 8
TILE = 384
CELL = 2 * TILE
PIECE = TF * TC
GW = 384
GH = GW // HD
TXT = 256
EXTRA = 16
COLUMNS = 1024
AXES = ("tm", "space")
SCALE = HD**-0.5 * math.log2(math.e)
MASKED = -1e30
TOO_FAR = 60.0 / SCALE
TEXT_LANE = 4
CONTRACT_LAST = (((1,), (1,)), ((), ()))


def device(y, z, x, c):
    return (2 * y + z % 2) * 16 + 8 * (z // 2) + 2 * x + c


PLACES = [(y, z, x, c) for y in range(4) for z in range(4) for x in range(4) for c in range(2)]
PLANES = [
    [device(y, z, x, c) for z in range(4) for x in range(4)] for y in range(4) for c in range(2)
]


SAME_PLACE = [
    [device(y, z, x, c) for y in range(4) for c in range(2)] for z in range(4) for x in range(4)
]


def route(target):
    pairs = []
    for place in PLACES:
        goal = target(*place)
        if goal is not None:
            pairs.append((device(*place), device(*goal)))
    return pairs


def to_other_chip(y, z, x, c):
    if c == 0:
        return (y - 1, z, x, 1) if y > 0 else None
    return (y + 1, z, x, 0) if y < 3 else None


OTHER_CHIP = route(to_other_chip)


def in_columns(steps):
    return route(lambda y, z, x, c: (y, z, x + steps, c) if 0 <= x + steps < 4 else None)


def to_owner(turn):
    def target(y, z, x, c):
        tile = (z + turn) % 4
        return (y, 2 * (x // 2) + c, 2 * (x % 2) + tile // 2, tile % 2)

    return route(target)


OTHER_CORE = route(lambda y, z, x, c: (y, z, x, 1 - c))


TIME_PARTNER = route(lambda y, z, x, c: (y, z ^ 1, x, c))


def send(value, pairs):
    return lax.ppermute(value, AXES, pairs)


def exchange(value, groups):
    return lax.all_to_all(
        value, AXES, split_axis=0, concat_axis=0, tiled=True, axis_index_groups=groups
    )


def pack_kernel(k_ref, v_ref, out_ref):
    for p in range(4):
        columns = slice(2 * TC * p, 2 * TC * (p + 1))
        for kind, ref in enumerate((k_ref, v_ref)):
            cut = ref[:, columns, :].astype(jnp.float32).reshape(TF, 2, TC, GW)
            for w in range(2):
                piece = cut[:, w].reshape(PIECE, GW).astype(jnp.bfloat16)
                out_ref[p, (2 * w + kind) * PIECE : (2 * w + kind + 1) * PIECE] = piece


def pack_queries_kernel(q_ref, text_ref, out_ref):
    for p in range(4):
        rows = q_ref[:, 2 * TC * p : 2 * TC * (p + 1), :].reshape(2 * PIECE, GW)
        out_ref[p, : 2 * PIECE] = rows
        out_ref[p, 2 * PIECE :] = text_ref[...]


def pack(kernel, rows, rasters, *text):
    raster = pl.BlockSpec((TF, 8 * TC, GW), lambda g: (0, 0, g))
    text_spec = pl.BlockSpec((PIECE, GW), lambda g: (0, g))
    return pl.pallas_call(
        kernel,
        grid=(4,),
        in_specs=[raster] * len(rasters) + [text_spec] * len(text),
        out_specs=pl.BlockSpec((4, rows, GW), lambda g: (g, 0, 0)),
        out_shape=jax.ShapeDtypeStruct((16, rows, GW), jnp.bfloat16),
        compiler_params=pltpu.CompilerParams(vmem_limit_bytes=56 * 2**20),
        cost_estimate=pl.CostEstimate(flops=0, bytes_accessed=16 * rows * GW * 4, transcendentals=0),
        name="pack",
    )(*[array.reshape(TF, 8 * TC, 4 * GW) for array in rasters], *text)


def copy_pieces(get, put):
    for x in range(4):
        for part in range(2):
            for w in range(2):
                for kind in range(2):
                    start = (2 * x + part) * PIECE
                    rows = slice((2 * w + kind) * PIECE, (2 * w + kind + 1) * PIECE)
                    put(kind, w, slice(start, start + PIECE), get(part, x, rows))


def merge_sides_kernel(c_ref, mine_ref, other_ref, low_ref, high_ref):
    parts, columns = (mine_ref, other_ref), (low_ref, high_ref)

    def put(kind, w, rows, value):
        columns[w][kind, rows] = value

    copy_pieces(lambda part, x, rows: parts[part][0, 0, x, rows], put)


def merge_kernel(c_ref, mine_ref, other_ref, own_ref, near_ref):
    parts = (mine_ref, other_ref)
    for place, out_ref in ((c_ref[0], own_ref), (1 - c_ref[0], near_ref)):

        def put(kind, w, rows, value, out_ref=out_ref):
            out_ref[kind, w, rows] = value

        copy_pieces(lambda part, x, rows, place=place: parts[part][0, place, x, rows], put)


def merge_queries_kernel(c_ref, mine_ref, other_ref, q_ref):
    even_core = c_ref[0] == 0
    for x in range(4):
        for f in range(TF):
            rows = slice(2 * TC * f, 2 * TC * (f + 1))
            mine = mine_ref[0, 0, x, rows].astype(jnp.float32)
            other = other_ref[0, x, rows].astype(jnp.float32)
            even = jnp.where(even_core, mine, other)
            odd = jnp.where(even_core, other, mine)
            start = (4 * f + x) * 2 * TC
            for w in range(2):
                both = [part[w * TC : (w + 1) * TC] for part in (even, odd)]
                q_ref[w, 0, start : start + 2 * TC] = jnp.concatenate(both).astype(jnp.bfloat16)


def merge(core, pieces, other, kernel, piece_specs, out_specs, out_shape):
    rows = pieces.shape[3]
    return pl.pallas_call(
        kernel,
        grid_spec=pltpu.PrefetchScalarGridSpec(
            num_scalar_prefetch=1, grid=(2,), in_specs=piece_specs, out_specs=out_specs
        ),
        out_shape=out_shape,
        compiler_params=pltpu.CompilerParams(vmem_limit_bytes=56 * 2**20),
        cost_estimate=pl.CostEstimate(flops=0, bytes_accessed=16 * rows * GW * 4, transcendentals=0),
        name="merge",
    )(core, pieces, other)


def merge_sides(core, pieces, other):
    piece = pl.BlockSpec((1, 1, 4, 4 * PIECE, GW), lambda b, c: (b, c[0], 0, 0, 0))
    cell = pl.BlockSpec((2, TILE, GW), lambda b, c: (0, b, 0))
    shape = jax.ShapeDtypeStruct((2, CELL, GW), jnp.bfloat16)
    return merge(
        core, pieces, other, merge_sides_kernel, [piece, piece], [cell, cell], [shape, shape]
    )


def merge_keys(core, pieces, other):
    piece = pl.BlockSpec((1, 2, 4, 4 * PIECE, GW), lambda b, c: (b, 0, 0, 0, 0))
    both = pl.BlockSpec((2, 2, TILE, GW), lambda b, c: (0, 0, b, 0))
    shape = jax.ShapeDtypeStruct((2, 2, CELL, GW), jnp.bfloat16)
    return merge(core, pieces, other, merge_kernel, [piece, piece], [both, both], [shape, shape])


def merge_queries(core, got):
    rows = got.shape[1]
    pieces = got.reshape(2, 2, 4, rows, GW)
    other = send(lax.dynamic_index_in_dim(pieces, 1 - core[0], 1, keepdims=False), OTHER_CORE)
    specs = [
        pl.BlockSpec((1, 1, 4, rows, GW), lambda b, c: (b, c[0], 0, 0, 0)),
        pl.BlockSpec((1, 4, rows, GW), lambda b, c: (b, 0, 0, 0)),
    ]
    spec = pl.BlockSpec((2, 1, TILE, GW), lambda b, c: (0, b, 0, 0))
    shape = jax.ShapeDtypeStruct((2, 2, TILE, GW), jnp.bfloat16)
    return merge(core, pieces, other, merge_queries_kernel, specs, spec, shape)


def join_kernel(left_ref, right_ref, out_ref):
    out_ref[:, 0] = left_ref[...]
    out_ref[:, 1] = right_ref[...]


def join(left, right):
    half = pl.BlockSpec((1, CELL, GW), lambda k: (k, 0, 0))
    return pl.pallas_call(
        join_kernel,
        grid=(2,),
        in_specs=[half, half],
        out_specs=pl.BlockSpec((1, 2, CELL, GW), lambda k: (k, 0, 0, 0)),
        out_shape=jax.ShapeDtypeStruct((2, 2, CELL, GW), jnp.bfloat16),
        compiler_params=pltpu.CompilerParams(vmem_limit_bytes=56 * 2**20),
        cost_estimate=pl.CostEstimate(flops=0, bytes_accessed=16 * CELL * GW, transcendentals=0),
        name="join",
    )(left, right)


def project_kernel(from_ref, first, second, third, fourth, weight_ref, out_ref, whole_ref):
    @pl.when(pl.program_id(0) == 0)
    def _():
        for i, ref in enumerate((first, second, third, fourth)):
            whole_ref[:, pl.ds(pl.multiple_of(from_ref[i] * GW, GW), GW)] = ref[...]

    columns = pl.ds(pl.multiple_of(pl.program_id(0) * COLUMNS, COLUMNS), COLUMNS)
    out_ref[...] = jnp.dot(
        whole_ref[...], weight_ref[:, columns], preferred_element_type=jnp.float32
    ).astype(jnp.bfloat16)


def project(groups, parts, weight):
    depth, width = weight.shape
    part = pl.BlockSpec((TILE, GW), lambda n, groups: (0, 0))
    return pl.pallas_call(
        project_kernel,
        grid_spec=pltpu.PrefetchScalarGridSpec(
            num_scalar_prefetch=1,
            grid=(width // COLUMNS,),
            in_specs=[part] * 4 + [pl.BlockSpec(memory_space=pltpu.VMEM)],
            out_specs=pl.BlockSpec((TILE, COLUMNS), lambda n, groups: (0, n)),
            scratch_shapes=[pltpu.VMEM((TILE, depth), jnp.bfloat16)],
        ),
        out_shape=jax.ShapeDtypeStruct((TILE, width), jnp.bfloat16),
        compiler_params=pltpu.CompilerParams(vmem_limit_bytes=24 * 2**20),
        cost_estimate=pl.CostEstimate(
            flops=2 * TILE * depth * width, bytes_accessed=2 * depth * width, transcendentals=0
        ),
        name="project",
    )(groups, *parts, weight)


def wide_bias(table):
    halves = [
        jnp.broadcast_to(table[b][None], (TILE // EXTRA, EXTRA, HD)).reshape(TILE, HD)
        for b in range(2)
    ]
    return jnp.concatenate(halves)


def add_keys(query, state, keys, bias, values):
    ones = jnp.ones((keys.shape[0], HD), jnp.bfloat16)
    scores = lax.dot_general(
        query,
        jnp.concatenate([keys, bias], axis=1),
        CONTRACT_LAST,
        preferred_element_type=jnp.float32,
    )
    top = jnp.max(scores, axis=1, keepdims=True)
    if state is not None:
        top = jnp.maximum(top, state[0])
    weights = jnp.exp2((scores - top) * SCALE).astype(jnp.bfloat16)
    part = jnp.dot(
        weights, jnp.concatenate([values, ones], axis=1), preferred_element_type=jnp.float32
    )
    if state is not None:
        part = part + state[1] * jnp.exp2((state[0] - top) * SCALE)
    return top, part


def add_all(query, state, blocks):
    for keys, bias, values in blocks:
        state = add_keys(query, state, keys(), wide_bias(bias()), values())
    return state, None


def add_all_late(query, state, blocks):
    peak, total = state
    step = None
    for keys, bias, values in blocks:
        scores = lax.dot_general(
            query,
            jnp.concatenate([keys(), wide_bias(bias())], axis=1),
            CONTRACT_LAST,
            preferred_element_type=jnp.float32,
        )
        weights = jnp.exp2((scores - peak) * SCALE).astype(jnp.bfloat16)
        ones = jnp.ones((CELL, HD), jnp.bfloat16)
        part = jnp.dot(
            weights, jnp.concatenate([values(), ones], axis=1), preferred_element_type=jnp.float32
        )
        top = jnp.maximum(peak, jnp.max(scores, axis=1, keepdims=True))
        rise = top - peak
        total = (total + part) * jnp.exp2(-rise * SCALE)
        step = rise if step is None else jnp.maximum(step, rise)
        peak = top
    return (peak, total), jnp.max(step)


def widened(query, first_lane):
    rows = query.shape[0]
    lanes = lax.broadcasted_iota(jnp.int32, (rows, HD), 1)
    which = lax.broadcasted_iota(jnp.int32, (rows, HD), 0) // TILE
    hot = jnp.where(lanes == first_lane + which, 1.0, 0.0).astype(jnp.bfloat16)
    return jnp.concatenate([query, hot], axis=1)


def mark_of(state):
    rows = state[1].shape[0]
    lanes = lax.broadcasted_iota(jnp.int32, (rows, HD), 1)
    return jnp.where(lanes < HD // 2, jnp.broadcast_to(state[0], (rows, HD)), state[1][:, HD:])


def near_kernel(cells, q_ref, tk_ref, tv_ref, bias_ref, *refs):
    sum_ref, mark_ref = refs[2 * cells :]

    def run(w, late):
        query = widened(q_ref[w].reshape(CELL, HD), 2 * w)
        no_bias = jnp.zeros((TXT, HD), jnp.bfloat16)
        state = add_keys(query, None, tk_ref[0], no_bias, tv_ref[0])
        blocks = [
            (
                functools.partial(refs[2 * (i // 2)].__getitem__, (0, i % 2)),
                functools.partial(bias_ref.__getitem__, i),
                functools.partial(refs[2 * (i // 2) + 1].__getitem__, (0, i % 2)),
            )
            for i in range(2 * cells)
        ]
        state, step = late(query, state, blocks)
        sum_ref[w] = state[1][:, :HD]
        mark_ref[w] = mark_of(state)
        return step

    step = jnp.maximum(run(0, add_all_late), run(1, add_all_late))

    @pl.when(step > TOO_FAR)
    def _():
        @pl.loop(0, 2)
        def _(w):
            run(w, add_all)


def cell_specs(number):
    def spec(kind):
        return pl.BlockSpec((1, 2, CELL, HD), lambda h: (kind, 0, 0, h))

    return [spec(0), spec(1)] * number


def doubled(cells):
    return [array for cell in cells for array in (cell, cell)]


def cost(rows, keys, heads):
    return pl.CostEstimate(
        flops=rows * keys * heads * 4 * 384,
        bytes_accessed=4 * keys * heads * HD,
        transcendentals=rows * keys * heads,
    )


def near(queries, text_all, bias, cells):
    state = pl.BlockSpec((2, CELL, HD), lambda h: (0, 0, h))
    shape = jax.ShapeDtypeStruct((2, CELL, GW), jnp.float32)
    return pl.pallas_call(
        functools.partial(near_kernel, len(cells)),
        grid=(GH,),
        in_specs=[
            pl.BlockSpec((2, 2, TILE, HD), lambda h: (0, 0, 0, h)),
            pl.BlockSpec((1, TXT, HD), lambda h: (1, 0, h)),
            pl.BlockSpec((1, TXT, HD), lambda h: (2, 0, h)),
            pl.BlockSpec(bias.shape, lambda h: (0, 0, 0, 0)),
        ]
        + cell_specs(len(cells)),
        out_specs=[state, state],
        out_shape=[shape, shape],
        compiler_params=pltpu.CompilerParams(vmem_limit_bytes=52 * 2**20),
        cost_estimate=cost(2 * CELL, 2 * len(cells) * CELL + TXT, GH),
        name="near_cells",
    )(queries, text_all, text_all, bias, *doubled(cells))


def side_kernel(valid_ref, q_ref, sum_ref, mark_ref, bias_ref, *refs):
    out_ref = refs[6]
    row = lax.broadcasted_iota(jnp.int32, (CELL, HD), 0)

    def run(w, late):
        query = widened(q_ref[w].reshape(CELL, HD), 2 * w)
        mark = mark_ref[w]
        totals = jnp.broadcast_to(mark[:, HD // 2 : HD // 2 + 1], (CELL, HD))
        state = (mark[:, :1], jnp.concatenate([sum_ref[w], totals], axis=1))
        blocks = [
            (
                functools.partial(refs[2 * i].__getitem__, (0, w)),
                functools.partial(bias_ref.__getitem__, 3 * w + i),
                functools.partial(refs[2 * i + 1].__getitem__, (0, w)),
            )
            for i in range(3)
        ]
        state, step = late(query, state, blocks)
        value = state[1][:, :HD] / state[1][:, HD:]
        value = jnp.where(row % TC < valid_ref[w], value, 0.0).astype(jnp.bfloat16)
        out_ref[w] = value.reshape(2, TILE, HD)
        return step

    step = jnp.maximum(run(0, add_all_late), run(1, add_all_late))

    @pl.when(step > TOO_FAR)
    def _():
        @pl.loop(0, 2)
        def _(w):
            run(w, add_all)


def side(valid, queries, state, bias, cells):
    tall = pl.BlockSpec((2, CELL, HD), lambda h: (0, 0, h))
    query = pl.BlockSpec((2, 2, TILE, HD), lambda h: (0, 0, 0, h))
    return pl.pallas_call(
        side_kernel,
        grid=(GH,),
        in_specs=[
            pl.BlockSpec(memory_space=pltpu.SMEM),
            query,
            tall,
            tall,
            pl.BlockSpec(bias.shape, lambda h: (0, 0, 0, 0)),
        ]
        + cell_specs(3),
        out_specs=query,
        out_shape=jax.ShapeDtypeStruct((2, 2, TILE, GW), jnp.bfloat16),
        compiler_params=pltpu.CompilerParams(vmem_limit_bytes=52 * 2**20),
        cost_estimate=cost(2 * CELL, 3 * CELL, GH),
        name="side_cells",
    )(valid, queries, *state, bias, *doubled(cells))


def text_kernel(share_ref, q_ref, tk_ref, tv_ref, bias_ref, *refs):
    out_ref = refs[2]
    head = pl.program_id(0)
    lanes = lax.broadcasted_iota(jnp.int32, (TXT, HD), 1)
    rows = lax.broadcasted_iota(jnp.int32, (TXT, HD), 0)
    hot = jnp.where(lanes == TEXT_LANE, 1.0, 0.0).astype(jnp.bfloat16)
    query = jnp.concatenate([q_ref[0], hot], axis=1)
    share = jnp.where(rows // 8 == share_ref[0], 0.0, MASKED).astype(jnp.bfloat16)
    state = None
    for i in range(2):
        bias = wide_bias(bias_ref[i])
        state = add_keys(query, state, refs[0][0, i], bias, refs[1][0, i])
    state = add_keys(query, state, tk_ref[0], share, tv_ref[0])
    out_ref[:, pl.ds(pl.multiple_of(head * HD, HD), HD)] = state[1][:, :HD]
    mark = jnp.where(
        lanes % 8 == head, jnp.where(lanes < 8, state[0], state[1][:, HD:]), 0.0
    )

    @pl.when(head == 0)
    def _():
        out_ref[:, GW:] = mark

    @pl.when(head > 0)
    def _():
        out_ref[:, GW:] += mark


def text_part(share, text_all, bias, cells):
    def spec(kind):
        return pl.BlockSpec((1, TXT, HD), lambda h: (kind, 0, h))

    return pl.pallas_call(
        text_kernel,
        grid=(GH,),
        in_specs=[
            pl.BlockSpec(memory_space=pltpu.SMEM),
            spec(0),
            spec(1),
            spec(2),
            pl.BlockSpec(bias.shape, lambda h: (0, 0, 0, 0)),
        ]
        + cell_specs(1),
        out_specs=pl.BlockSpec((TXT, GW + HD), lambda h: (0, 0)),
        out_shape=jax.ShapeDtypeStruct((TXT, GW + HD), jnp.float32),
        compiler_params=pltpu.CompilerParams(vmem_limit_bytes=56 * 2**20),
        cost_estimate=cost(TXT, 2 * CELL + TXT, GH),
        name="text_queries",
    )(share, text_all, text_all, text_all, bias, *doubled(cells))


def text_sum_kernel(part_ref, out_ref):
    for z in range(4):
        marks = part_ref[:, z % 2, z // 2, :, :, GW:]
        top = jnp.max(marks, axis=(0, 1), keepdims=True)
        factors = jnp.exp2((marks - top) * SCALE)
        for h in range(GH):
            factor = factors[..., h : h + 1]
            total = jnp.sum(marks[..., 8 + h : 9 + h] * factor, axis=(0, 1))
            part = part_ref[:, z % 2, z // 2, :, :, h * HD : (h + 1) * HD]
            summed = jnp.sum(part * factor, axis=(0, 1)) / total
            start = z * GW + h * HD
            out_ref[:, start : start + HD] = summed.astype(jnp.bfloat16)


def text_sum(parts):
    return pl.pallas_call(
        text_sum_kernel,
        out_shape=jax.ShapeDtypeStruct((2, 4 * GW), jnp.bfloat16),
        compiler_params=pltpu.CompilerParams(vmem_limit_bytes=56 * 2**20),
        cost_estimate=pl.CostEstimate(
            flops=0, bytes_accessed=TXT * (GW + HD) * 4, transcendentals=0
        ),
        name="text_sum",
    )(parts.reshape(4, 2, 2, 8, 2, GW + HD))


def shards(
    video_query,
    video_key,
    video_value,
    text_query,
    text_key,
    text_value,
    window_lists,
    valid_columns,
    video_weight,
    text_weight,
):
    tm, space = lax.axis_index("tm"), lax.axis_index("space")
    y, zl = tm // 2, tm % 2
    zh, x, c = space // 8, space // 2 % 4, space % 2
    z = 2 * zh + zl
    moment = 2 * y + c

    packed = pack(pack_kernel, 4 * PIECE, [video_key, video_value])
    packed, lists = lax.optimization_barrier((packed, window_lists))
    got = exchange(packed, PLANES)

    other_lists = send(lists, TIME_PARTNER)
    text_rows = jnp.concatenate([text_query, text_key, text_value], axis=0)
    text_some = lax.all_gather(text_rows, AXES, axis_index_groups=SAME_PLACE, tiled=True)
    packed_queries = pack(pack_queries_kernel, 3 * PIECE, [video_query], text_some)
    got, packed_queries = lax.optimization_barrier((got, packed_queries))

    core = c.reshape(1)
    pieces = got.reshape(2, 2, 4, 4 * PIECE, GW)
    other = send(pieces, OTHER_CORE)
    low, high = merge_sides(core, pieces, other)

    left, right = send(high, in_columns(1)), send(low, in_columns(-1))
    other, _ = lax.optimization_barrier((other, low))
    own, beside = merge_keys(core, pieces, other)
    beyond = send(own, OTHER_CHIP)

    got_queries = exchange(packed_queries, PLANES)
    queries = merge_queries(core, got_queries)

    text_all = got_queries[:, 2 * PIECE :].reshape(2, 2, 4, 4, 2, 3, 2, GW)
    text_all = text_all.transpose(5, 3, 1, 0, 2, 4, 6, 7).reshape(3, TXT, GW)

    got_lists = jnp.where(zl == c, lists, other_lists).reshape(2, 8, 27)
    tile_lists = lax.dynamic_slice_in_dim(got_lists, 2 * x, 2, 1).transpose(1, 0, 2).reshape(4, 27)
    key_moment = moment + jnp.arange(-1, 2, dtype=jnp.int32)[:, None, None]
    key_column = 2 * x + jnp.arange(-1, 3, dtype=jnp.int32)[None, :, None]
    key_band = jnp.arange(2, dtype=jnp.int32)[None, None, :]
    inside = (key_moment >= 0) & (key_moment < 8) & (key_column >= 0) & (key_column < 8)
    idents = jnp.where(inside, 16 * key_moment + 8 * key_band + key_column, -2)
    listed = jnp.any(idents[..., None, None] == tile_lists, axis=-1)
    places = jnp.arange(8, dtype=jnp.int32)
    columns = 2 * x + jnp.arange(-1, 3, dtype=jnp.int32)
    valid = jnp.sum(
        jnp.where(places[None, :] == columns[:, None], valid_columns[None, :], 0), axis=1
    )
    fine = (jnp.arange(EXTRA, dtype=jnp.int32) % TC)[None, :] < valid[:, None]
    listed = jnp.pad(listed, ((0, 0), (0, 0), (0, 0), (0, HD - 4)), constant_values=True)
    allowed = listed[:, :, :, None, :] & fine[None, :, None, :, None]
    bias = jnp.where(allowed, 0.0, MASKED).astype(jnp.bfloat16)
    even_core = c == 0
    beside_bias = jnp.where(even_core, bias[2], bias[0])
    beyond_bias = jnp.where(even_core, bias[0], bias[2])
    bias = jnp.stack([bias[1], beside_bias, beyond_bias])
    near_bias = bias[:, 1:3].reshape(6, 2, EXTRA, HD)
    side_bias = jnp.concatenate([bias[:, 0], bias[:, 3]])

    member = (4 * y + x) * 2 + c
    parts = text_part(member.reshape(1), text_all, near_bias[:2], [own])
    left, right, _, queries = lax.optimization_barrier((left, right, parts, queries))
    parts = exchange(parts.reshape(128, 2, GW + HD), None)
    sides = join(left, right)
    beside_sides, beyond_sides = send(sides, OTHER_CORE), send(sides, OTHER_CHIP)

    state = near(queries, text_all, near_bias, [own, beside, beyond])
    attended = side(valid[1:3], queries, state, side_bias, [sides, beside_sides, beyond_sides])
    parts, attended = lax.optimization_barrier((parts, attended))
    attended = attended.reshape(4, TILE, GW)

    turns = jnp.arange(4, dtype=jnp.int32)
    arrived = [
        send(lax.dynamic_index_in_dim(attended, (z + turn) % 4, 0, keepdims=False), to_owner(turn))
        for turn in range(4)
    ]
    video_output = project((2 * (x % 2) + c - turns) % 4, arrived, video_weight)
    video_output = video_output.reshape(1, 1, 1, TILE, -1)
    text_attn = text_sum(parts)
    text_output = jnp.dot(text_attn, text_weight, preferred_element_type=jnp.float32)
    text_output = text_output.astype(jnp.bfloat16)
    return (video_output, text_output)


def solution(mesh):
    in_specs = (
        P("tm", "space", None, None),
        P("tm", "space", None, None),
        P("tm", "space", None, None),
        P(("tm", "space"), None),
        P(("tm", "space"), None),
        P(("tm", "space"), None),
        P("tm", None, None),
        P(),
        P(),
        P(),
    )
    out_specs = (P("tm", "space", None, None, None), P(("tm", "space"), None))
    return jax.shard_map(shards, mesh=mesh, in_specs=in_specs, out_specs=out_specs, check_vma=False)
```

```python
import functools
import math

import jax
import jax.numpy as jnp
from jax import lax
from jax.experimental import pallas as pl
from jax.experimental.pallas import tpu as pltpu
from jax.sharding import PartitionSpec as P

HD = 128
TF = 6
TC = 8
TILE = 384
CELL = 2 * TILE
PIECE = TF * TC
GW = 384
GH = GW // HD
TXT = 256
EXTRA = 16
COLUMNS = 1024
AXES = ("tm", "space")
SCALE = HD**-0.5 * math.log2(math.e)
MASKED = -1e30
TOO_FAR = 60.0 / SCALE
TEXT_LANE = 4
CONTRACT_LAST = (((1,), (1,)), ((), ()))


def device(y, z, x, c):
    return (2 * y + z % 2) * 16 + 8 * (z // 2) + 2 * x + c


PLACES = [(y, z, x, c) for y in range(4) for z in range(4) for x in range(4) for c in range(2)]
PLANES = [
    [device(y, z, x, c) for z in range(4) for x in range(4)] for y in range(4) for c in range(2)
]


SAME_PLACE = [
    [device(y, z, x, c) for y in range(4) for c in range(2)] for z in range(4) for x in range(4)
]


EVERYONE = [
    [device(y, z, x, c) for z in range(4) for x in range(4) for y in range(4) for c in range(2)]
]


def route(target):
    pairs = []
    for place in PLACES:
        goal = target(*place)
        if goal is not None:
            pairs.append((device(*place), device(*goal)))
    return pairs


def to_other_chip(y, z, x, c):
    if c == 0:
        return (y - 1, z, x, 1) if y > 0 else None
    return (y + 1, z, x, 0) if y < 3 else None


OTHER_CHIP = route(to_other_chip)


def in_columns(steps):
    return route(lambda y, z, x, c: (y, z, x + steps, c) if 0 <= x + steps < 4 else None)


def to_owner(turn):
    def target(y, z, x, c):
        tile = (z + turn) % 4
        return (y, 2 * (x // 2) + c, 2 * (x % 2) + tile // 2, tile % 2)

    return route(target)


OTHER_CORE = route(lambda y, z, x, c: (y, z, x, 1 - c))


TIME_PARTNER = route(lambda y, z, x, c: (y, z ^ 1, x, c))


def send(value, pairs):
    return lax.ppermute(value, AXES, pairs)


def exchange(value, groups):
    return lax.all_to_all(
        value, AXES, split_axis=0, concat_axis=0, tiled=True, axis_index_groups=groups
    )


def pack_kernel(k_ref, v_ref, out_ref):
    for p in range(4):
        columns = slice(2 * TC * p, 2 * TC * (p + 1))
        for kind, ref in enumerate((k_ref, v_ref)):
            cut = ref[:, columns, :].astype(jnp.float32).reshape(TF, 2, TC, GW)
            for w in range(2):
                piece = cut[:, w].reshape(PIECE, GW).astype(jnp.bfloat16)
                out_ref[p, (2 * w + kind) * PIECE : (2 * w + kind + 1) * PIECE] = piece


def pack_queries_kernel(q_ref, text_ref, out_ref):
    for p in range(4):
        rows = q_ref[:, 2 * TC * p : 2 * TC * (p + 1), :].reshape(2 * PIECE, GW)
        out_ref[p, : 2 * PIECE] = rows
        out_ref[p, 2 * PIECE :] = text_ref[...]


def pack(kernel, rows, rasters, *text):
    raster = pl.BlockSpec((TF, 8 * TC, GW), lambda g: (0, 0, g))
    text_spec = pl.BlockSpec((PIECE, GW), lambda g: (0, g))
    return pl.pallas_call(
        kernel,
        grid=(4,),
        in_specs=[raster] * len(rasters) + [text_spec] * len(text),
        out_specs=pl.BlockSpec((4, rows, GW), lambda g: (g, 0, 0)),
        out_shape=jax.ShapeDtypeStruct((16, rows, GW), jnp.bfloat16),
        compiler_params=pltpu.CompilerParams(vmem_limit_bytes=56 * 2**20),
        cost_estimate=pl.CostEstimate(flops=0, bytes_accessed=16 * rows * GW * 4, transcendentals=0),
        name="pack",
    )(*[array.reshape(TF, 8 * TC, 4 * GW) for array in rasters], *text)


def copy_pieces(get, put):
    for x in range(4):
        for part in range(2):
            for w in range(2):
                for kind in range(2):
                    start = (2 * x + part) * PIECE
                    rows = slice((2 * w + kind) * PIECE, (2 * w + kind + 1) * PIECE)
                    put(kind, w, slice(start, start + PIECE), get(part, x, rows))


def merge_kernel(c_ref, mine_ref, other_ref, low_ref, high_ref, own_ref, beside_ref):
    parts, columns = (mine_ref, other_ref), (low_ref, high_ref)
    place = c_ref[0]

    def put(kind, w, rows, value):
        columns[w][kind, rows] = value
        own_ref[kind, w, rows] = value

    def put_beside(kind, w, rows, value):
        beside_ref[kind, w, rows] = value

    copy_pieces(lambda part, x, rows: parts[part][0, place, x, rows], put)
    copy_pieces(lambda part, x, rows: parts[part][0, 1 - place, x, rows], put_beside)


def merge_queries_kernel(c_ref, mine_ref, other_ref, rows_ref, q_ref, text_ref):
    even_core = c_ref[0] == 0

    @pl.when(pl.program_id(0) == 0)
    def _():
        for source in range(16):
            for kind in range(3):
                rows = rows_ref[source, 16 * kind : 16 * (kind + 1)]
                text_ref[kind, 16 * source : 16 * (source + 1)] = rows

    for x in range(4):
        for f in range(TF):
            rows = slice(2 * TC * f, 2 * TC * (f + 1))
            mine = mine_ref[0, 0, x, rows].astype(jnp.float32)
            other = other_ref[0, x, rows].astype(jnp.float32)
            even = jnp.where(even_core, mine, other)
            odd = jnp.where(even_core, other, mine)
            start = (4 * f + x) * 2 * TC
            for w in range(2):
                both = [part[w * TC : (w + 1) * TC] for part in (even, odd)]
                q_ref[w, 0, start : start + 2 * TC] = jnp.concatenate(both).astype(jnp.bfloat16)


def merge(core, arrays, kernel, piece_specs, out_specs, out_shape):
    size = sum(math.prod(shape.shape) for shape in out_shape)
    return pl.pallas_call(
        kernel,
        grid_spec=pltpu.PrefetchScalarGridSpec(
            num_scalar_prefetch=1, grid=(2,), in_specs=piece_specs, out_specs=out_specs
        ),
        out_shape=out_shape,
        compiler_params=pltpu.CompilerParams(vmem_limit_bytes=56 * 2**20),
        cost_estimate=pl.CostEstimate(flops=0, bytes_accessed=4 * size, transcendentals=0),
        name="merge",
    )(core, *arrays)


def merge_keys(core, pieces, other):
    piece = pl.BlockSpec((1, 2, 4, 4 * PIECE, GW), lambda b, c: (b, 0, 0, 0, 0))
    cell = pl.BlockSpec((2, TILE, GW), lambda b, c: (0, b, 0))
    shape = jax.ShapeDtypeStruct((2, CELL, GW), jnp.bfloat16)
    both = pl.BlockSpec((2, 2, TILE, GW), lambda b, c: (0, 0, b, 0))
    both_shape = jax.ShapeDtypeStruct((2, 2, CELL, GW), jnp.bfloat16)
    specs, shapes = [cell, cell, both, both], [shape, shape, both_shape, both_shape]
    return merge(core, [pieces, other], merge_kernel, [piece, piece], specs, shapes)


def merge_queries(core, got):
    pieces = got.reshape(2, 2, 4, 3 * PIECE, GW)
    leaving = pieces[:, :, :, : 2 * PIECE]
    other = send(lax.dynamic_index_in_dim(leaving, 1 - core[0], 1, keepdims=False), OTHER_CORE)
    specs = [
        pl.BlockSpec((1, 1, 4, 2 * PIECE, GW), lambda b, c: (b, c[0], 0, 0, 0)),
        pl.BlockSpec((1, 4, 2 * PIECE, GW), lambda b, c: (b, 0, 0, 0)),
        pl.BlockSpec((16, PIECE, GW), lambda b, c: (0, 2, 0)),
    ]
    out_specs = [
        pl.BlockSpec((2, 1, TILE, GW), lambda b, c: (0, b, 0, 0)),
        pl.BlockSpec((3, TXT, GW), lambda b, c: (0, 0, 0)),
    ]
    shapes = [
        jax.ShapeDtypeStruct((2, 2, TILE, GW), jnp.bfloat16),
        jax.ShapeDtypeStruct((3, TXT, GW), jnp.bfloat16),
    ]
    return merge(core, [pieces, other, got], merge_queries_kernel, specs, out_specs, shapes)


def join_kernel(left_ref, right_ref, out_ref):
    out_ref[:, 0] = left_ref[...]
    out_ref[:, 1] = right_ref[...]


def join(left, right):
    half = pl.BlockSpec((1, CELL, GW), lambda k: (k, 0, 0))
    return pl.pallas_call(
        join_kernel,
        grid=(2,),
        in_specs=[half, half],
        out_specs=pl.BlockSpec((1, 2, CELL, GW), lambda k: (k, 0, 0, 0)),
        out_shape=jax.ShapeDtypeStruct((2, 2, CELL, GW), jnp.bfloat16),
        compiler_params=pltpu.CompilerParams(vmem_limit_bytes=56 * 2**20),
        cost_estimate=pl.CostEstimate(flops=0, bytes_accessed=16 * CELL * GW, transcendentals=0),
        name="join",
    )(left, right)


def project_kernel(from_ref, first, second, third, fourth, weight_ref, out_ref, whole_ref):
    @pl.when(pl.program_id(0) == 0)
    def _():
        for i, ref in enumerate((first, second, third, fourth)):
            whole_ref[:, pl.ds(pl.multiple_of(from_ref[i] * GW, GW), GW)] = ref[...]

    columns = pl.ds(pl.multiple_of(pl.program_id(0) * COLUMNS, COLUMNS), COLUMNS)
    out_ref[...] = jnp.dot(
        whole_ref[...], weight_ref[:, columns], preferred_element_type=jnp.float32
    ).astype(jnp.bfloat16)


def project(groups, parts, weight):
    depth, width = weight.shape
    part = pl.BlockSpec((TILE, GW), lambda n, groups: (0, 0))
    return pl.pallas_call(
        project_kernel,
        grid_spec=pltpu.PrefetchScalarGridSpec(
            num_scalar_prefetch=1,
            grid=(width // COLUMNS,),
            in_specs=[part] * 4 + [pl.BlockSpec(memory_space=pltpu.VMEM)],
            out_specs=pl.BlockSpec((TILE, COLUMNS), lambda n, groups: (0, n)),
            scratch_shapes=[pltpu.VMEM((TILE, depth), jnp.bfloat16)],
        ),
        out_shape=jax.ShapeDtypeStruct((TILE, width), jnp.bfloat16),
        compiler_params=pltpu.CompilerParams(vmem_limit_bytes=24 * 2**20),
        cost_estimate=pl.CostEstimate(
            flops=2 * TILE * depth * width, bytes_accessed=2 * depth * width, transcendentals=0
        ),
        name="project",
    )(groups, *parts, weight)


def wide_bias(table):
    halves = [
        jnp.broadcast_to(table[b][None], (TILE // EXTRA, EXTRA, HD)).reshape(TILE, HD)
        for b in range(2)
    ]
    return jnp.concatenate(halves)


def add_keys(query, state, keys, bias, values):
    ones = jnp.ones((keys.shape[0], HD), jnp.bfloat16)
    scores = lax.dot_general(
        query,
        jnp.concatenate([keys, bias], axis=1),
        CONTRACT_LAST,
        preferred_element_type=jnp.float32,
    )
    top = jnp.max(scores, axis=1, keepdims=True)
    if state is not None:
        top = jnp.maximum(top, state[0])
    weights = jnp.exp2((scores - top) * SCALE).astype(jnp.bfloat16)
    part = jnp.dot(
        weights, jnp.concatenate([values, ones], axis=1), preferred_element_type=jnp.float32
    )
    if state is not None:
        part = part + state[1] * jnp.exp2((state[0] - top) * SCALE)
    return top, part


def add_all(query, state, blocks):
    for keys, bias, values in blocks:
        state = add_keys(query, state, keys(), wide_bias(bias()), values())
    return state, None


def add_all_late(query, state, blocks):
    peak, total = state
    step = None
    for keys, bias, values in blocks:
        scores = lax.dot_general(
            query,
            jnp.concatenate([keys(), wide_bias(bias())], axis=1),
            CONTRACT_LAST,
            preferred_element_type=jnp.float32,
        )
        weights = jnp.exp2((scores - peak) * SCALE).astype(jnp.bfloat16)
        ones = jnp.ones((CELL, HD), jnp.bfloat16)
        part = jnp.dot(
            weights, jnp.concatenate([values(), ones], axis=1), preferred_element_type=jnp.float32
        )
        top = jnp.maximum(peak, jnp.max(scores, axis=1, keepdims=True))
        rise = top - peak
        total = (total + part) * jnp.exp2(-rise * SCALE)
        step = rise if step is None else jnp.maximum(step, rise)
        peak = top
    return (peak, total), jnp.max(step)


def widened(query, first_lane):
    rows = query.shape[0]
    lanes = lax.broadcasted_iota(jnp.int32, (rows, HD), 1)
    which = lax.broadcasted_iota(jnp.int32, (rows, HD), 0) // TILE
    hot = jnp.where(lanes == first_lane + which, 1.0, 0.0).astype(jnp.bfloat16)
    return jnp.concatenate([query, hot], axis=1)


def mark_of(state):
    rows = state[1].shape[0]
    lanes = lax.broadcasted_iota(jnp.int32, (rows, HD), 1)
    return jnp.where(lanes < HD // 2, jnp.broadcast_to(state[0], (rows, HD)), state[1][:, HD:])


def near_kernel(cells, q_ref, tk_ref, tv_ref, bias_ref, *refs):
    sum_ref, mark_ref = refs[2 * cells :]

    def run(w, late):
        query = widened(q_ref[w].reshape(CELL, HD), 2 * w)
        no_bias = jnp.zeros((TXT, HD), jnp.bfloat16)
        state = add_keys(query, None, tk_ref[0], no_bias, tv_ref[0])
        blocks = [
            (
                functools.partial(refs[2 * (i // 2)].__getitem__, (0, i % 2)),
                functools.partial(bias_ref.__getitem__, i),
                functools.partial(refs[2 * (i // 2) + 1].__getitem__, (0, i % 2)),
            )
            for i in range(2 * cells)
        ]
        state, step = late(query, state, blocks)
        sum_ref[w] = state[1][:, :HD]
        mark_ref[w] = mark_of(state)
        return step

    step = jnp.maximum(run(0, add_all_late), run(1, add_all_late))

    @pl.when(step > TOO_FAR)
    def _():
        @pl.loop(0, 2)
        def _(w):
            run(w, add_all)


def cell_specs(number):
    def spec(kind):
        return pl.BlockSpec((1, 2, CELL, HD), lambda h: (kind, 0, 0, h))

    return [spec(0), spec(1)] * number


def doubled(cells):
    return [array for cell in cells for array in (cell, cell)]


def cost(rows, keys, heads):
    return pl.CostEstimate(
        flops=rows * keys * heads * 4 * 384,
        bytes_accessed=4 * keys * heads * HD,
        transcendentals=rows * keys * heads,
    )


def near(queries, text_all, bias, cells):
    state = pl.BlockSpec((2, CELL, HD), lambda h: (0, 0, h))
    shape = jax.ShapeDtypeStruct((2, CELL, GW), jnp.float32)
    return pl.pallas_call(
        functools.partial(near_kernel, len(cells)),
        grid=(GH,),
        in_specs=[
            pl.BlockSpec((2, 2, TILE, HD), lambda h: (0, 0, 0, h)),
            pl.BlockSpec((1, TXT, HD), lambda h: (1, 0, h)),
            pl.BlockSpec((1, TXT, HD), lambda h: (2, 0, h)),
            pl.BlockSpec(bias.shape, lambda h: (0, 0, 0, 0)),
        ]
        + cell_specs(len(cells)),
        out_specs=[state, state],
        out_shape=[shape, shape],
        compiler_params=pltpu.CompilerParams(vmem_limit_bytes=52 * 2**20),
        cost_estimate=cost(2 * CELL, 2 * len(cells) * CELL + TXT, GH),
        name="near_cells",
    )(queries, text_all, text_all, bias, *doubled(cells))


def side_kernel(valid_ref, q_ref, sum_ref, mark_ref, bias_ref, *refs):
    out_ref = refs[6]
    row = lax.broadcasted_iota(jnp.int32, (CELL, HD), 0)

    def run(w, late):
        query = widened(q_ref[w].reshape(CELL, HD), 2 * w)
        mark = mark_ref[w]
        totals = jnp.broadcast_to(mark[:, HD // 2 : HD // 2 + 1], (CELL, HD))
        state = (mark[:, :1], jnp.concatenate([sum_ref[w], totals], axis=1))
        blocks = [
            (
                functools.partial(refs[2 * i].__getitem__, (0, w)),
                functools.partial(bias_ref.__getitem__, 3 * w + i),
                functools.partial(refs[2 * i + 1].__getitem__, (0, w)),
            )
            for i in range(3)
        ]
        state, step = late(query, state, blocks)
        value = state[1][:, :HD] / state[1][:, HD:]
        value = jnp.where(row % TC < valid_ref[w], value, 0.0).astype(jnp.bfloat16)
        out_ref[w] = value.reshape(2, TILE, HD)
        return step

    step = jnp.maximum(run(0, add_all_late), run(1, add_all_late))

    @pl.when(step > TOO_FAR)
    def _():
        @pl.loop(0, 2)
        def _(w):
            run(w, add_all)


def side(valid, queries, state, bias, cells):
    tall = pl.BlockSpec((2, CELL, HD), lambda h: (0, 0, h))
    query = pl.BlockSpec((2, 2, TILE, HD), lambda h: (0, 0, 0, h))
    return pl.pallas_call(
        side_kernel,
        grid=(GH,),
        in_specs=[
            pl.BlockSpec(memory_space=pltpu.SMEM),
            query,
            tall,
            tall,
            pl.BlockSpec(bias.shape, lambda h: (0, 0, 0, 0)),
        ]
        + cell_specs(3),
        out_specs=query,
        out_shape=jax.ShapeDtypeStruct((2, 2, TILE, GW), jnp.bfloat16),
        compiler_params=pltpu.CompilerParams(vmem_limit_bytes=52 * 2**20),
        cost_estimate=cost(2 * CELL, 3 * CELL, GH),
        name="side_cells",
    )(valid, queries, *state, bias, *doubled(cells))


def text_kernel(share_ref, q_ref, tk_ref, tv_ref, bias_ref, *refs):
    out_ref = refs[2]
    head = pl.program_id(0)
    lanes = lax.broadcasted_iota(jnp.int32, (TXT, HD), 1)
    rows = lax.broadcasted_iota(jnp.int32, (TXT, HD), 0)
    hot = jnp.where(lanes == TEXT_LANE, 1.0, 0.0).astype(jnp.bfloat16)
    query = jnp.concatenate([q_ref[0], hot], axis=1)
    share = jnp.where(rows // 8 == share_ref[0], 0.0, MASKED).astype(jnp.bfloat16)
    state = None
    for i in range(2):
        bias = wide_bias(bias_ref[i])
        state = add_keys(query, state, refs[0][0, i], bias, refs[1][0, i])
    state = add_keys(query, state, tk_ref[0], share, tv_ref[0])
    out_ref[:, pl.ds(pl.multiple_of(head * HD, HD), HD)] = state[1][:, :HD]
    mark = jnp.where(
        lanes % 8 == head, jnp.where(lanes < 8, state[0], state[1][:, HD:]), 0.0
    )

    @pl.when(head == 0)
    def _():
        out_ref[:, GW:] = mark

    @pl.when(head > 0)
    def _():
        out_ref[:, GW:] += mark


def text_part(share, text_all, bias, cells):
    def spec(kind):
        return pl.BlockSpec((1, TXT, HD), lambda h: (kind, 0, h))

    return pl.pallas_call(
        text_kernel,
        grid=(GH,),
        in_specs=[
            pl.BlockSpec(memory_space=pltpu.SMEM),
            spec(0),
            spec(1),
            spec(2),
            pl.BlockSpec(bias.shape, lambda h: (0, 0, 0, 0)),
        ]
        + cell_specs(1),
        out_specs=pl.BlockSpec((TXT, GW + HD), lambda h: (0, 0)),
        out_shape=jax.ShapeDtypeStruct((TXT, GW + HD), jnp.float32),
        compiler_params=pltpu.CompilerParams(vmem_limit_bytes=56 * 2**20),
        cost_estimate=cost(TXT, 2 * CELL + TXT, GH),
        name="text_queries",
    )(share, text_all, text_all, text_all, bias, *doubled(cells))


def text_sum_kernel(part_ref, out_ref):
    for z in range(4):
        marks = part_ref[z, :, :, GW:]
        top = jnp.max(marks, axis=0, keepdims=True)
        factors = jnp.exp2((marks - top) * SCALE)
        for h in range(GH):
            factor = factors[..., h : h + 1]
            total = jnp.sum(marks[..., 8 + h : 9 + h] * factor, axis=0)
            part = part_ref[z, :, :, h * HD : (h + 1) * HD]
            summed = jnp.sum(part * factor, axis=0) / total
            start = z * GW + h * HD
            out_ref[:, start : start + HD] = summed.astype(jnp.bfloat16)


def text_sum(parts):
    return pl.pallas_call(
        text_sum_kernel,
        out_shape=jax.ShapeDtypeStruct((2, 4 * GW), jnp.bfloat16),
        compiler_params=pltpu.CompilerParams(vmem_limit_bytes=56 * 2**20),
        cost_estimate=pl.CostEstimate(
            flops=0, bytes_accessed=TXT * (GW + HD) * 4, transcendentals=0
        ),
        name="text_sum",
    )(parts.reshape(4, 32, 2, GW + HD))


def shards(
    video_query,
    video_key,
    video_value,
    text_query,
    text_key,
    text_value,
    window_lists,
    valid_columns,
    video_weight,
    text_weight,
):
    tm, space = lax.axis_index("tm"), lax.axis_index("space")
    y, zl = tm // 2, tm % 2
    zh, x, c = space // 8, space // 2 % 4, space % 2
    z = 2 * zh + zl
    moment = 2 * y + c

    packed = pack(pack_kernel, 4 * PIECE, [video_key, video_value])
    packed, lists = lax.optimization_barrier((packed, window_lists))
    got = exchange(packed, PLANES)

    other_lists = send(lists, TIME_PARTNER)
    text_rows = jnp.concatenate([text_query, text_key, text_value], axis=0)
    text_some = lax.all_gather(text_rows, AXES, axis_index_groups=SAME_PLACE, tiled=True)
    text_some = text_some.reshape(8, 3, 2, 4 * GW).transpose(1, 0, 2, 3).reshape(PIECE, 4 * GW)
    packed_queries = pack(pack_queries_kernel, 3 * PIECE, [video_query], text_some)
    got, packed_queries = lax.optimization_barrier((got, packed_queries))

    core = c.reshape(1)
    pieces = got.reshape(2, 2, 4, 4 * PIECE, GW)
    other = send(pieces, OTHER_CORE)
    low, high, own, beside = merge_keys(core, pieces, other)

    left, right = send(high, in_columns(1)), send(low, in_columns(-1))
    beyond = send(own, OTHER_CHIP)

    got_queries = exchange(packed_queries, PLANES)
    queries, text_all = merge_queries(core, got_queries)

    got_lists = jnp.where(zl == c, lists, other_lists).reshape(2, 8, 27)
    tile_lists = lax.dynamic_slice_in_dim(got_lists, 2 * x, 2, 1).transpose(1, 0, 2).reshape(4, 27)
    key_moment = moment + jnp.arange(-1, 2, dtype=jnp.int32)[:, None, None]
    key_column = 2 * x + jnp.arange(-1, 3, dtype=jnp.int32)[None, :, None]
    key_band = jnp.arange(2, dtype=jnp.int32)[None, None, :]
    inside = (key_moment >= 0) & (key_moment < 8) & (key_column >= 0) & (key_column < 8)
    idents = jnp.where(inside, 16 * key_moment + 8 * key_band + key_column, -2)
    listed = jnp.any(idents[..., None, None] == tile_lists, axis=-1)
    places = jnp.arange(8, dtype=jnp.int32)
    columns = 2 * x + jnp.arange(-1, 3, dtype=jnp.int32)
    valid = jnp.sum(
        jnp.where(places[None, :] == columns[:, None], valid_columns[None, :], 0), axis=1
    )
    fine = (jnp.arange(EXTRA, dtype=jnp.int32) % TC)[None, :] < valid[:, None]
    listed = jnp.pad(listed, ((0, 0), (0, 0), (0, 0), (0, HD - 4)), constant_values=True)
    allowed = listed[:, :, :, None, :] & fine[None, :, None, :, None]
    bias = jnp.where(allowed, 0.0, MASKED).astype(jnp.bfloat16)
    even_core = c == 0
    beside_bias = jnp.where(even_core, bias[2], bias[0])
    beyond_bias = jnp.where(even_core, bias[0], bias[2])
    bias = jnp.stack([bias[1], beside_bias, beyond_bias])
    near_bias = bias[:, 1:3].reshape(6, 2, EXTRA, HD)
    side_bias = jnp.concatenate([bias[:, 0], bias[:, 3]])

    member = (4 * y + x) * 2 + c
    parts = text_part(member.reshape(1), text_all, near_bias[:2], [own])
    left, right, _, queries = lax.optimization_barrier((left, right, parts, queries))
    parts = exchange(parts.reshape(128, 2, GW + HD), EVERYONE)
    sides = join(left, right)
    beside_sides, beyond_sides = send(sides, OTHER_CORE), send(sides, OTHER_CHIP)

    state = near(queries, text_all, near_bias, [own, beside, beyond])
    attended = side(valid[1:3], queries, state, side_bias, [sides, beside_sides, beyond_sides])
    parts, attended = lax.optimization_barrier((parts, attended))
    attended = attended.reshape(4, TILE, GW)

    turns = jnp.arange(4, dtype=jnp.int32)
    arrived = [
        send(lax.dynamic_index_in_dim(attended, (z + turn) % 4, 0, keepdims=False), to_owner(turn))
        for turn in range(4)
    ]
    video_output = project((2 * (x % 2) + c - turns) % 4, arrived, video_weight)
    video_output = video_output.reshape(1, 1, 1, TILE, -1)
    text_attn = text_sum(parts)
    text_output = jnp.dot(text_attn, text_weight, preferred_element_type=jnp.float32)
    text_output = text_output.astype(jnp.bfloat16)
    return (video_output, text_output)


def solution(mesh):
    in_specs = (
        P("tm", "space", None, None),
        P("tm", "space", None, None),
        P("tm", "space", None, None),
        P(("tm", "space"), None),
        P(("tm", "space"), None),
        P(("tm", "space"), None),
        P("tm", None, None),
        P(),
        P(),
        P(),
    )
    out_specs = (P("tm", "space", None, None, None), P(("tm", "space"), None))
    return jax.shard_map(shards, mesh=mesh, in_specs=in_specs, out_specs=out_specs, check_vma=False)
```

```python
import functools
import math

import jax
import jax.numpy as jnp
from jax import lax
from jax.experimental import pallas as pl
from jax.experimental.pallas import tpu as pltpu
from jax.sharding import PartitionSpec as P

HD = 128
TF = 6
TC = 8
TILE = 384
CELL = 2 * TILE
PIECE = TF * TC
GW = 384
GH = GW // HD
TXT = 256
EXTRA = 16
COLUMNS = 1024
AXES = ("tm", "space")
SCALE = HD**-0.5 * math.log2(math.e)
MASKED = -1e30
TOO_FAR = 60.0 / SCALE
TEXT_LANE = 4
CONTRACT_LAST = (((1,), (1,)), ((), ()))


def device(y, z, x, c):
    return (2 * y + z % 2) * 16 + 8 * (z // 2) + 2 * x + c


PLACES = [(y, z, x, c) for y in range(4) for z in range(4) for x in range(4) for c in range(2)]
PLANES = [
    [device(y, z, x, c) for z in range(4) for x in range(4)] for y in range(4) for c in range(2)
]


SAME_PLACE = [
    [device(y, z, x, c) for y in range(4) for c in range(2)] for z in range(4) for x in range(4)
]


EVERYONE = [
    [device(y, z, x, c) for z in range(4) for x in range(4) for y in range(4) for c in range(2)]
]


def route(target):
    pairs = []
    for place in PLACES:
        goal = target(*place)
        if goal is not None:
            pairs.append((device(*place), device(*goal)))
    return pairs


def to_other_chip(y, z, x, c):
    if c == 0:
        return (y - 1, z, x, 1) if y > 0 else None
    return (y + 1, z, x, 0) if y < 3 else None


OTHER_CHIP = route(to_other_chip)


def in_columns(steps):
    return route(lambda y, z, x, c: (y, z, x + steps, c) if 0 <= x + steps < 4 else None)


def to_owner(turn):
    def target(y, z, x, c):
        tile = (z + turn) % 4
        return (y, 2 * (x // 2) + c, 2 * (x % 2) + tile // 2, tile % 2)

    return route(target)


OTHER_CORE = route(lambda y, z, x, c: (y, z, x, 1 - c))


TIME_PARTNER = route(lambda y, z, x, c: (y, z ^ 1, x, c))


def send(value, pairs):
    return lax.ppermute(value, AXES, pairs)


def exchange(value, groups):
    return lax.all_to_all(
        value, AXES, split_axis=0, concat_axis=0, tiled=True, axis_index_groups=groups
    )


def pack_kernel(k_ref, v_ref, out_ref):
    for p in range(4):
        columns = slice(2 * TC * p, 2 * TC * (p + 1))
        for kind, ref in enumerate((k_ref, v_ref)):
            cut = ref[:, columns, :].astype(jnp.float32).reshape(TF, 2, TC, GW)
            for w in range(2):
                piece = cut[:, w].reshape(PIECE, GW).astype(jnp.bfloat16)
                out_ref[p, (2 * w + kind) * PIECE : (2 * w + kind + 1) * PIECE] = piece


def pack_queries_kernel(q_ref, text_ref, out_ref):
    for p in range(4):
        rows = q_ref[:, 2 * TC * p : 2 * TC * (p + 1), :].reshape(2 * PIECE, GW)
        out_ref[p, : 2 * PIECE] = rows
        out_ref[p, 2 * PIECE :] = text_ref[...]


def pack(kernel, rows, rasters, *text):
    raster = pl.BlockSpec((TF, 8 * TC, GW), lambda g: (0, 0, g))
    text_spec = pl.BlockSpec((PIECE, GW), lambda g: (0, g))
    return pl.pallas_call(
        kernel,
        grid=(4,),
        in_specs=[raster] * len(rasters) + [text_spec] * len(text),
        out_specs=pl.BlockSpec((4, rows, GW), lambda g: (g, 0, 0)),
        out_shape=jax.ShapeDtypeStruct((16, rows, GW), jnp.bfloat16),
        compiler_params=pltpu.CompilerParams(vmem_limit_bytes=56 * 2**20),
        cost_estimate=pl.CostEstimate(flops=0, bytes_accessed=16 * rows * GW * 4, transcendentals=0),
        name="pack",
    )(*[array.reshape(TF, 8 * TC, 4 * GW) for array in rasters], *text)


def copy_pieces(get, put):
    for x in range(4):
        for part in range(2):
            for w in range(2):
                for kind in range(2):
                    start = (2 * x + part) * PIECE
                    rows = slice((2 * w + kind) * PIECE, (2 * w + kind + 1) * PIECE)
                    put(kind, w, slice(start, start + PIECE), get(part, x, rows))


def merge_kernel(c_ref, mine_ref, other_ref, low_ref, high_ref, own_ref, beside_ref):
    parts, columns = (mine_ref, other_ref), (low_ref, high_ref)
    place = c_ref[0]

    def put(kind, w, rows, value):
        columns[w][kind, rows] = value
        own_ref[kind, w, rows] = value

    def put_beside(kind, w, rows, value):
        beside_ref[kind, w, rows] = value

    copy_pieces(lambda part, x, rows: parts[part][0, place, x, rows], put)
    copy_pieces(lambda part, x, rows: parts[part][0, 1 - place, x, rows], put_beside)


def merge_queries_kernel(c_ref, mine_ref, other_ref, rows_ref, q_ref, text_ref):
    even_core = c_ref[0] == 0

    @pl.when(pl.program_id(0) == 0)
    def _():
        for source in range(16):
            for kind in range(3):
                rows = rows_ref[source, 16 * kind : 16 * (kind + 1)]
                text_ref[kind, 16 * source : 16 * (source + 1)] = rows

    for x in range(4):
        for f in range(TF):
            rows = slice(2 * TC * f, 2 * TC * (f + 1))
            mine = mine_ref[0, 0, x, rows].astype(jnp.float32)
            other = other_ref[0, x, rows].astype(jnp.float32)
            even = jnp.where(even_core, mine, other)
            odd = jnp.where(even_core, other, mine)
            start = (4 * f + x) * 2 * TC
            for w in range(2):
                both = [part[w * TC : (w + 1) * TC] for part in (even, odd)]
                q_ref[w, 0, start : start + 2 * TC] = jnp.concatenate(both).astype(jnp.bfloat16)


def merge(core, arrays, kernel, piece_specs, out_specs, out_shape):
    size = sum(math.prod(shape.shape) for shape in out_shape)
    return pl.pallas_call(
        kernel,
        grid_spec=pltpu.PrefetchScalarGridSpec(
            num_scalar_prefetch=1, grid=(2,), in_specs=piece_specs, out_specs=out_specs
        ),
        out_shape=out_shape,
        compiler_params=pltpu.CompilerParams(vmem_limit_bytes=56 * 2**20),
        cost_estimate=pl.CostEstimate(flops=0, bytes_accessed=4 * size, transcendentals=0),
        name="merge",
    )(core, *arrays)


def merge_keys(core, pieces, other):
    piece = pl.BlockSpec((1, 2, 4, 4 * PIECE, GW), lambda b, c: (b, 0, 0, 0, 0))
    cell = pl.BlockSpec((2, TILE, GW), lambda b, c: (0, b, 0))
    shape = jax.ShapeDtypeStruct((2, CELL, GW), jnp.bfloat16)
    both = pl.BlockSpec((2, 2, TILE, GW), lambda b, c: (0, 0, b, 0))
    both_shape = jax.ShapeDtypeStruct((2, 2, CELL, GW), jnp.bfloat16)
    specs, shapes = [cell, cell, both, both], [shape, shape, both_shape, both_shape]
    return merge(core, [pieces, other], merge_kernel, [piece, piece], specs, shapes)


def merge_queries(core, got):
    pieces = got.reshape(2, 2, 4, 3 * PIECE, GW)
    leaving = pieces[:, :, :, : 2 * PIECE]
    other = send(lax.dynamic_index_in_dim(leaving, 1 - core[0], 1, keepdims=False), OTHER_CORE)
    specs = [
        pl.BlockSpec((1, 1, 4, 2 * PIECE, GW), lambda b, c: (b, c[0], 0, 0, 0)),
        pl.BlockSpec((1, 4, 2 * PIECE, GW), lambda b, c: (b, 0, 0, 0)),
        pl.BlockSpec((16, PIECE, GW), lambda b, c: (0, 2, 0)),
    ]
    out_specs = [
        pl.BlockSpec((2, 1, TILE, GW), lambda b, c: (0, b, 0, 0)),
        pl.BlockSpec((3, TXT, GW), lambda b, c: (0, 0, 0)),
    ]
    shapes = [
        jax.ShapeDtypeStruct((2, 2, TILE, GW), jnp.bfloat16),
        jax.ShapeDtypeStruct((3, TXT, GW), jnp.bfloat16),
    ]
    return merge(core, [pieces, other, got], merge_queries_kernel, specs, out_specs, shapes)


def join_kernel(left_ref, right_ref, out_ref):
    out_ref[:, 0] = left_ref[...]
    out_ref[:, 1] = right_ref[...]


def join(left, right):
    half = pl.BlockSpec((1, CELL, GW), lambda k: (k, 0, 0))
    return pl.pallas_call(
        join_kernel,
        grid=(2,),
        in_specs=[half, half],
        out_specs=pl.BlockSpec((1, 2, CELL, GW), lambda k: (k, 0, 0, 0)),
        out_shape=jax.ShapeDtypeStruct((2, 2, CELL, GW), jnp.bfloat16),
        compiler_params=pltpu.CompilerParams(vmem_limit_bytes=56 * 2**20),
        cost_estimate=pl.CostEstimate(flops=0, bytes_accessed=16 * CELL * GW, transcendentals=0),
        name="join",
    )(left, right)


def project_kernel(from_ref, first, second, third, fourth, weight_ref, out_ref, whole_ref):
    @pl.when(pl.program_id(0) == 0)
    def _():
        for i, ref in enumerate((first, second, third, fourth)):
            whole_ref[:, pl.ds(pl.multiple_of(from_ref[i] * GW, GW), GW)] = ref[...]

    columns = pl.ds(pl.multiple_of(pl.program_id(0) * COLUMNS, COLUMNS), COLUMNS)
    out_ref[...] = jnp.dot(
        whole_ref[...], weight_ref[:, columns], preferred_element_type=jnp.float32
    ).astype(jnp.bfloat16)


def project(groups, parts, weight):
    depth, width = weight.shape
    part = pl.BlockSpec((TILE, GW), lambda n, groups: (0, 0))
    return pl.pallas_call(
        project_kernel,
        grid_spec=pltpu.PrefetchScalarGridSpec(
            num_scalar_prefetch=1,
            grid=(width // COLUMNS,),
            in_specs=[part] * 4 + [pl.BlockSpec(memory_space=pltpu.VMEM)],
            out_specs=pl.BlockSpec((TILE, COLUMNS), lambda n, groups: (0, n)),
            scratch_shapes=[pltpu.VMEM((TILE, depth), jnp.bfloat16)],
        ),
        out_shape=jax.ShapeDtypeStruct((TILE, width), jnp.bfloat16),
        compiler_params=pltpu.CompilerParams(vmem_limit_bytes=24 * 2**20),
        cost_estimate=pl.CostEstimate(
            flops=2 * TILE * depth * width, bytes_accessed=2 * depth * width, transcendentals=0
        ),
        name="project",
    )(groups, *parts, weight)


def wide_bias(table):
    halves = [
        jnp.broadcast_to(table[b][None], (TILE // EXTRA, EXTRA, HD)).reshape(TILE, HD)
        for b in range(2)
    ]
    return jnp.concatenate(halves)


def add_keys(query, state, keys, bias, values):
    ones = jnp.ones((keys.shape[0], HD), jnp.bfloat16)
    scores = lax.dot_general(
        query,
        jnp.concatenate([keys, bias], axis=1),
        CONTRACT_LAST,
        preferred_element_type=jnp.float32,
    )
    top = jnp.max(scores, axis=1, keepdims=True)
    if state is not None:
        top = jnp.maximum(top, state[0])
    weights = jnp.exp2((scores - top) * SCALE).astype(jnp.bfloat16)
    part = jnp.dot(
        weights, jnp.concatenate([values, ones], axis=1), preferred_element_type=jnp.float32
    )
    if state is not None:
        part = part + state[1] * jnp.exp2((state[0] - top) * SCALE)
    return top, part


def add_all(query, state, blocks):
    for keys, bias, values in blocks:
        state = add_keys(query, state, keys(), wide_bias(bias()), values())
    return state, None


def add_all_late(query, state, blocks):
    peak, total = state
    step = None
    for keys, bias, values in blocks:
        scores = lax.dot_general(
            query,
            jnp.concatenate([keys(), wide_bias(bias())], axis=1),
            CONTRACT_LAST,
            preferred_element_type=jnp.float32,
        )
        weights = jnp.exp2((scores - peak) * SCALE).astype(jnp.bfloat16)
        ones = jnp.ones((CELL, HD), jnp.bfloat16)
        part = jnp.dot(
            weights, jnp.concatenate([values(), ones], axis=1), preferred_element_type=jnp.float32
        )
        top = jnp.maximum(peak, jnp.max(scores, axis=1, keepdims=True))
        rise = top - peak
        total = (total + part) * jnp.exp2(-rise * SCALE)
        step = rise if step is None else jnp.maximum(step, rise)
        peak = top
    return (peak, total), jnp.max(step)


def widened(query, first_lane):
    rows = query.shape[0]
    lanes = lax.broadcasted_iota(jnp.int32, (rows, HD), 1)
    which = lax.broadcasted_iota(jnp.int32, (rows, HD), 0) // TILE
    hot = jnp.where(lanes == first_lane + which, 1.0, 0.0).astype(jnp.bfloat16)
    return jnp.concatenate([query, hot], axis=1)


def lanes_of(rows):
    return lax.broadcasted_iota(jnp.int32, (rows, HD), 1)


def near_kernel(cells, q_ref, tk_ref, tv_ref, bias_ref, *refs):
    sum_ref, mark_ref = refs[2 * cells :]

    def run(w, late):
        query = widened(q_ref[w].reshape(CELL, HD), 2 * w)
        no_bias = jnp.zeros((TXT, HD), jnp.bfloat16)
        state = add_keys(query, None, tk_ref[0], no_bias, tv_ref[0])
        blocks = [
            (
                functools.partial(refs[2 * (i // 2)].__getitem__, (0, i % 2)),
                functools.partial(bias_ref.__getitem__, i),
                functools.partial(refs[2 * (i // 2) + 1].__getitem__, (0, i % 2)),
            )
            for i in range(2 * cells)
        ]
        state, step = late(query, state, blocks)
        sum_ref[w] = state[1][:, :HD]
        lanes, head = lanes_of(CELL), pl.program_id(0)
        mark = jnp.where(lanes < 8, jnp.broadcast_to(state[0], (CELL, HD)), state[1][:, HD:])
        others = jnp.where(head == 0, 0.0, mark_ref[w])
        mark_ref[w] = jnp.where(lanes % 8 == head, mark, others)
        return step

    step = jnp.maximum(run(0, add_all_late), run(1, add_all_late))

    @pl.when(step > TOO_FAR)
    def _():
        @pl.loop(0, 2)
        def _(w):
            run(w, add_all)


def cell_specs(number):
    def spec(kind):
        return pl.BlockSpec((1, 2, CELL, HD), lambda h: (kind, 0, 0, h))

    return [spec(0), spec(1)] * number


def doubled(cells):
    return [array for cell in cells for array in (cell, cell)]


def cost(rows, keys, heads):
    return pl.CostEstimate(
        flops=rows * keys * heads * 4 * 384,
        bytes_accessed=4 * keys * heads * HD,
        transcendentals=rows * keys * heads,
    )


def near(queries, text_all, bias, cells):
    state = pl.BlockSpec((2, CELL, HD), lambda h: (0, 0, h))
    shape = jax.ShapeDtypeStruct((2, CELL, GW), jnp.float32)
    return pl.pallas_call(
        functools.partial(near_kernel, len(cells)),
        grid=(GH,),
        in_specs=[
            pl.BlockSpec((2, 2, TILE, HD), lambda h: (0, 0, 0, h)),
            pl.BlockSpec((1, TXT, HD), lambda h: (1, 0, h)),
            pl.BlockSpec((1, TXT, HD), lambda h: (2, 0, h)),
            pl.BlockSpec(bias.shape, lambda h: (0, 0, 0, 0)),
        ]
        + cell_specs(len(cells)),
        out_specs=[state, pl.BlockSpec((2, CELL, HD), lambda h: (0, 0, 0))],
        out_shape=[shape, jax.ShapeDtypeStruct((2, CELL, HD), jnp.float32)],
        compiler_params=pltpu.CompilerParams(vmem_limit_bytes=52 * 2**20),
        cost_estimate=cost(2 * CELL, 2 * len(cells) * CELL + TXT, GH),
        name="near_cells",
    )(queries, text_all, text_all, bias, *doubled(cells))


def side_kernel(valid_ref, q_ref, sum_ref, mark_ref, bias_ref, *refs):
    out_ref = refs[6]
    row = lax.broadcasted_iota(jnp.int32, (CELL, HD), 0)

    def run(w, late):
        query = widened(q_ref[w].reshape(CELL, HD), 2 * w)
        mark = mark_ref[w]
        lanes, head = lanes_of(CELL), pl.program_id(0)
        peak = jnp.sum(jnp.where(lanes == head, mark, 0.0), axis=1, keepdims=True)
        total = jnp.sum(jnp.where(lanes == 8 + head, mark, 0.0), axis=1, keepdims=True)
        totals = jnp.broadcast_to(total, (CELL, HD))
        state = (peak, jnp.concatenate([sum_ref[w], totals], axis=1))
        blocks = [
            (
                functools.partial(refs[2 * i].__getitem__, (0, w)),
                functools.partial(bias_ref.__getitem__, 3 * w + i),
                functools.partial(refs[2 * i + 1].__getitem__, (0, w)),
            )
            for i in range(3)
        ]
        state, step = late(query, state, blocks)
        value = state[1][:, :HD] / state[1][:, HD:]
        value = jnp.where(row % TC < valid_ref[w], value, 0.0).astype(jnp.bfloat16)
        out_ref[w] = value.reshape(2, TILE, HD)
        return step

    step = jnp.maximum(run(0, add_all_late), run(1, add_all_late))

    @pl.when(step > TOO_FAR)
    def _():
        @pl.loop(0, 2)
        def _(w):
            run(w, add_all)


def side(valid, queries, state, bias, cells):
    tall = pl.BlockSpec((2, CELL, HD), lambda h: (0, 0, h))
    query = pl.BlockSpec((2, 2, TILE, HD), lambda h: (0, 0, 0, h))
    return pl.pallas_call(
        side_kernel,
        grid=(GH,),
        in_specs=[
            pl.BlockSpec(memory_space=pltpu.SMEM),
            query,
            tall,
            pl.BlockSpec((2, CELL, HD), lambda h: (0, 0, 0)),
            pl.BlockSpec(bias.shape, lambda h: (0, 0, 0, 0)),
        ]
        + cell_specs(3),
        out_specs=query,
        out_shape=jax.ShapeDtypeStruct((2, 2, TILE, GW), jnp.bfloat16),
        compiler_params=pltpu.CompilerParams(vmem_limit_bytes=52 * 2**20),
        cost_estimate=cost(2 * CELL, 3 * CELL, GH),
        name="side_cells",
    )(valid, queries, *state, bias, *doubled(cells))


def text_kernel(share_ref, q_ref, tk_ref, tv_ref, bias_ref, *refs):
    out_ref = refs[2]
    head = pl.program_id(0)
    lanes = lax.broadcasted_iota(jnp.int32, (TXT, HD), 1)
    rows = lax.broadcasted_iota(jnp.int32, (TXT, HD), 0)
    hot = jnp.where(lanes == TEXT_LANE, 1.0, 0.0).astype(jnp.bfloat16)
    query = jnp.concatenate([q_ref[0], hot], axis=1)
    share = jnp.where(rows // 8 == share_ref[0], 0.0, MASKED).astype(jnp.bfloat16)
    state = None
    for i in range(2):
        bias = wide_bias(bias_ref[i])
        state = add_keys(query, state, refs[0][0, i], bias, refs[1][0, i])
    state = add_keys(query, state, tk_ref[0], share, tv_ref[0])
    out_ref[:, pl.ds(pl.multiple_of(head * HD, HD), HD)] = state[1][:, :HD]
    mark = jnp.where(
        lanes % 8 == head, jnp.where(lanes < 8, state[0], state[1][:, HD:]), 0.0
    )

    @pl.when(head == 0)
    def _():
        out_ref[:, GW:] = mark

    @pl.when(head > 0)
    def _():
        out_ref[:, GW:] += mark


def text_part(share, text_all, bias, cells):
    def spec(kind):
        return pl.BlockSpec((1, TXT, HD), lambda h: (kind, 0, h))

    return pl.pallas_call(
        text_kernel,
        grid=(GH,),
        in_specs=[
            pl.BlockSpec(memory_space=pltpu.SMEM),
            spec(0),
            spec(1),
            spec(2),
            pl.BlockSpec(bias.shape, lambda h: (0, 0, 0, 0)),
        ]
        + cell_specs(1),
        out_specs=pl.BlockSpec((TXT, GW + HD), lambda h: (0, 0)),
        out_shape=jax.ShapeDtypeStruct((TXT, GW + HD), jnp.float32),
        compiler_params=pltpu.CompilerParams(vmem_limit_bytes=56 * 2**20),
        cost_estimate=cost(TXT, 2 * CELL + TXT, GH),
        name="text_queries",
    )(share, text_all, text_all, text_all, bias, *doubled(cells))


def text_sum_kernel(part_ref, out_ref):
    for z in range(4):
        marks = part_ref[z, :, :, GW:]
        top = jnp.max(marks, axis=0, keepdims=True)
        factors = jnp.exp2((marks - top) * SCALE)
        for h in range(GH):
            factor = factors[..., h : h + 1]
            total = jnp.sum(marks[..., 8 + h : 9 + h] * factor, axis=0)
            part = part_ref[z, :, :, h * HD : (h + 1) * HD]
            summed = jnp.sum(part * factor, axis=0) / total
            start = z * GW + h * HD
            out_ref[:, start : start + HD] = summed.astype(jnp.bfloat16)


def text_sum(parts):
    return pl.pallas_call(
        text_sum_kernel,
        out_shape=jax.ShapeDtypeStruct((2, 4 * GW), jnp.bfloat16),
        compiler_params=pltpu.CompilerParams(vmem_limit_bytes=56 * 2**20),
        cost_estimate=pl.CostEstimate(
            flops=0, bytes_accessed=TXT * (GW + HD) * 4, transcendentals=0
        ),
        name="text_sum",
    )(parts.reshape(4, 32, 2, GW + HD))


def shards(
    video_query,
    video_key,
    video_value,
    text_query,
    text_key,
    text_value,
    window_lists,
    valid_columns,
    video_weight,
    text_weight,
):
    tm, space = lax.axis_index("tm"), lax.axis_index("space")
    y, zl = tm // 2, tm % 2
    zh, x, c = space // 8, space // 2 % 4, space % 2
    z = 2 * zh + zl
    moment = 2 * y + c

    packed = pack(pack_kernel, 4 * PIECE, [video_key, video_value])
    packed, lists = lax.optimization_barrier((packed, window_lists))
    got = exchange(packed, PLANES)

    other_lists = send(lists, TIME_PARTNER)
    text_rows = jnp.concatenate([text_query, text_key, text_value], axis=0)
    text_some = lax.all_gather(text_rows, AXES, axis_index_groups=SAME_PLACE, tiled=True)
    text_some = text_some.reshape(8, 3, 2, 4 * GW).transpose(1, 0, 2, 3).reshape(PIECE, 4 * GW)
    packed_queries = pack(pack_queries_kernel, 3 * PIECE, [video_query], text_some)
    got, packed_queries = lax.optimization_barrier((got, packed_queries))

    core = c.reshape(1)
    pieces = got.reshape(2, 2, 4, 4 * PIECE, GW)
    other = send(pieces, OTHER_CORE)
    low, high, own, beside = merge_keys(core, pieces, other)

    left, right = send(high, in_columns(1)), send(low, in_columns(-1))
    beyond = send(own, OTHER_CHIP)

    got_queries = exchange(packed_queries, PLANES)
    queries, text_all = merge_queries(core, got_queries)

    got_lists = jnp.where(zl == c, lists, other_lists).reshape(2, 8, 27)
    tile_lists = lax.dynamic_slice_in_dim(got_lists, 2 * x, 2, 1).transpose(1, 0, 2).reshape(4, 27)
    key_moment = moment + jnp.arange(-1, 2, dtype=jnp.int32)[:, None, None]
    key_column = 2 * x + jnp.arange(-1, 3, dtype=jnp.int32)[None, :, None]
    key_band = jnp.arange(2, dtype=jnp.int32)[None, None, :]
    inside = (key_moment >= 0) & (key_moment < 8) & (key_column >= 0) & (key_column < 8)
    idents = jnp.where(inside, 16 * key_moment + 8 * key_band + key_column, -2)
    listed = jnp.any(idents[..., None, None] == tile_lists, axis=-1)
    places = jnp.arange(8, dtype=jnp.int32)
    columns = 2 * x + jnp.arange(-1, 3, dtype=jnp.int32)
    valid = jnp.sum(
        jnp.where(places[None, :] == columns[:, None], valid_columns[None, :], 0), axis=1
    )
    fine = (jnp.arange(EXTRA, dtype=jnp.int32) % TC)[None, :] < valid[:, None]
    listed = jnp.pad(listed, ((0, 0), (0, 0), (0, 0), (0, HD - 4)), constant_values=True)
    allowed = listed[:, :, :, None, :] & fine[None, :, None, :, None]
    bias = jnp.where(allowed, 0.0, MASKED).astype(jnp.bfloat16)
    even_core = c == 0
    beside_bias = jnp.where(even_core, bias[2], bias[0])
    beyond_bias = jnp.where(even_core, bias[0], bias[2])
    bias = jnp.stack([bias[1], beside_bias, beyond_bias])
    near_bias = bias[:, 1:3].reshape(6, 2, EXTRA, HD)
    side_bias = jnp.concatenate([bias[:, 0], bias[:, 3]])

    member = (4 * y + x) * 2 + c
    parts = text_part(member.reshape(1), text_all, near_bias[:2], [own])
    left, right, _, queries = lax.optimization_barrier((left, right, parts, queries))
    parts = exchange(parts.reshape(128, 2, GW + HD), EVERYONE)
    sides = join(left, right)
    beside_sides, beyond_sides = send(sides, OTHER_CORE), send(sides, OTHER_CHIP)

    state = near(queries, text_all, near_bias, [own, beside, beyond])
    attended = side(valid[1:3], queries, state, side_bias, [sides, beside_sides, beyond_sides])
    parts, attended = lax.optimization_barrier((parts, attended))
    attended = attended.reshape(4, TILE, GW)

    turns = jnp.arange(4, dtype=jnp.int32)
    arrived = [
        send(lax.dynamic_index_in_dim(attended, (z + turn) % 4, 0, keepdims=False), to_owner(turn))
        for turn in range(4)
    ]
    video_output = project((2 * (x % 2) + c - turns) % 4, arrived, video_weight)
    video_output = video_output.reshape(1, 1, 1, TILE, -1)
    text_attn = text_sum(parts)
    text_output = jnp.dot(text_attn, text_weight, preferred_element_type=jnp.float32)
    text_output = text_output.astype(jnp.bfloat16)
    return (video_output, text_output)


def solution(mesh):
    in_specs = (
        P("tm", "space", None, None),
        P("tm", "space", None, None),
        P("tm", "space", None, None),
        P(("tm", "space"), None),
        P(("tm", "space"), None),
        P(("tm", "space"), None),
        P("tm", None, None),
        P(),
        P(),
        P(),
    )
    out_specs = (P("tm", "space", None, None, None), P(("tm", "space"), None))
    return jax.shard_map(shards, mesh=mesh, in_specs=in_specs, out_specs=out_specs, check_vma=False)
```

```python
import functools
import math

import jax
import jax.numpy as jnp
from jax import lax
from jax.experimental import pallas as pl
from jax.experimental.pallas import tpu as pltpu
from jax.sharding import PartitionSpec as P

HD = 128
TF = 6
TC = 8
TILE = 384
CELL = 2 * TILE
PIECE = TF * TC
GW = 384
GH = GW // HD
TXT = 256
EXTRA = 16
COLUMNS = 1024
AXES = ("tm", "space")
SCALE = HD**-0.5 * math.log2(math.e)
MASKED = -1e30
TOO_FAR = 60.0 / SCALE
TEXT_LANE = 4
CONTRACT_LAST = (((1,), (1,)), ((), ()))


def device(y, z, x, c):
    return (2 * y + z % 2) * 16 + 8 * (z // 2) + 2 * x + c


PLACES = [(y, z, x, c) for y in range(4) for z in range(4) for x in range(4) for c in range(2)]
PLANES = [
    [device(y, z, x, c) for z in range(4) for x in range(4)] for y in range(4) for c in range(2)
]


SAME_PLACE = [
    [device(y, z, x, c) for y in range(4) for c in range(2)] for z in range(4) for x in range(4)
]


EVERYONE = [
    [device(y, z, x, c) for z in range(4) for x in range(4) for y in range(4) for c in range(2)]
]


def route(target):
    pairs = []
    for place in PLACES:
        goal = target(*place)
        if goal is not None:
            pairs.append((device(*place), device(*goal)))
    return pairs


def to_other_chip(y, z, x, c):
    if c == 0:
        return (y - 1, z, x, 1) if y > 0 else None
    return (y + 1, z, x, 0) if y < 3 else None


OTHER_CHIP = route(to_other_chip)


def in_columns(steps):
    return route(lambda y, z, x, c: (y, z, x + steps, c) if 0 <= x + steps < 4 else None)


def to_owner(turn):
    def target(y, z, x, c):
        tile = (z + turn) % 4
        return (y, 2 * (x // 2) + c, 2 * (x % 2) + tile // 2, tile % 2)

    return route(target)


OTHER_CORE = route(lambda y, z, x, c: (y, z, x, 1 - c))


TIME_PARTNER = route(lambda y, z, x, c: (y, z ^ 1, x, c))


def send(value, pairs):
    return lax.ppermute(value, AXES, pairs)


def exchange(value, groups):
    return lax.all_to_all(
        value, AXES, split_axis=0, concat_axis=0, tiled=True, axis_index_groups=groups
    )


def pack_kernel(k_ref, v_ref, out_ref):
    for p in range(2):
        columns = slice(2 * TC * p, 2 * TC * (p + 1))
        for kind, ref in enumerate((k_ref, v_ref)):
            cut = ref[:, columns, :].astype(jnp.float32).reshape(TF, 2, TC, GW)
            for w in range(2):
                piece = cut[:, w].reshape(PIECE, GW).astype(jnp.bfloat16)
                out_ref[p, (2 * w + kind) * PIECE : (2 * w + kind + 1) * PIECE] = piece


def pack_queries_kernel(q_ref, text_ref, out_ref):
    for p in range(2):
        rows = q_ref[:, 2 * TC * p : 2 * TC * (p + 1), :].reshape(2 * PIECE, GW)
        out_ref[p, : 2 * PIECE] = rows
        out_ref[p, 2 * PIECE :] = text_ref[...]


def pack(kernel, rows, rasters, *text):
    raster = pl.BlockSpec((TF, 4 * TC, GW), lambda g, half: (0, half, g))
    text_spec = pl.BlockSpec((PIECE, GW), lambda g, half: (0, g))
    return pl.pallas_call(
        kernel,
        grid=(4, 2),
        in_specs=[raster] * len(rasters) + [text_spec] * len(text),
        out_specs=pl.BlockSpec((2, rows, GW), lambda g, half: (2 * g + half, 0, 0)),
        out_shape=jax.ShapeDtypeStruct((16, rows, GW), jnp.bfloat16),
        compiler_params=pltpu.CompilerParams(vmem_limit_bytes=56 * 2**20),
        cost_estimate=pl.CostEstimate(flops=0, bytes_accessed=16 * rows * GW * 4, transcendentals=0),
        name="pack",
    )(*[array.reshape(TF, 8 * TC, 4 * GW) for array in rasters], *text)


def copy_pieces(get, put):
    for x in range(4):
        for part in range(2):
            for w in range(2):
                for kind in range(2):
                    start = (2 * x + part) * PIECE
                    rows = slice((2 * w + kind) * PIECE, (2 * w + kind + 1) * PIECE)
                    put(kind, w, slice(start, start + PIECE), get(part, x, rows))


def merge_kernel(c_ref, mine_ref, other_ref, low_ref, high_ref, own_ref, beside_ref):
    parts, columns = (mine_ref, other_ref), (low_ref, high_ref)
    place = c_ref[0]

    def put(kind, w, rows, value):
        columns[w][kind, rows] = value
        own_ref[kind, w, rows] = value

    def put_beside(kind, w, rows, value):
        beside_ref[kind, w, rows] = value

    copy_pieces(lambda part, x, rows: parts[part][0, place, x, rows], put)
    copy_pieces(lambda part, x, rows: parts[part][0, 1 - place, x, rows], put_beside)


def merge_queries_kernel(c_ref, mine_ref, other_ref, rows_ref, q_ref, text_ref):
    even_core = c_ref[0] == 0

    @pl.when(pl.program_id(0) == 0)
    def _():
        for source in range(16):
            for kind in range(3):
                rows = rows_ref[source, 16 * kind : 16 * (kind + 1)]
                text_ref[kind, 16 * source : 16 * (source + 1)] = rows

    for x in range(4):
        for f in range(TF):
            rows = slice(2 * TC * f, 2 * TC * (f + 1))
            mine = mine_ref[0, 0, x, rows].astype(jnp.float32)
            other = other_ref[0, x, rows].astype(jnp.float32)
            even = jnp.where(even_core, mine, other)
            odd = jnp.where(even_core, other, mine)
            start = (4 * f + x) * 2 * TC
            for w in range(2):
                both = [part[w * TC : (w + 1) * TC] for part in (even, odd)]
                q_ref[w, 0, start : start + 2 * TC] = jnp.concatenate(both).astype(jnp.bfloat16)


def merge(core, arrays, kernel, piece_specs, out_specs, out_shape):
    size = sum(math.prod(shape.shape) for shape in out_shape)
    return pl.pallas_call(
        kernel,
        grid_spec=pltpu.PrefetchScalarGridSpec(
            num_scalar_prefetch=1, grid=(2,), in_specs=piece_specs, out_specs=out_specs
        ),
        out_shape=out_shape,
        compiler_params=pltpu.CompilerParams(vmem_limit_bytes=56 * 2**20),
        cost_estimate=pl.CostEstimate(flops=0, bytes_accessed=4 * size, transcendentals=0),
        name="merge",
    )(core, *arrays)


def merge_keys(core, pieces, other):
    piece = pl.BlockSpec((1, 2, 4, 4 * PIECE, GW), lambda b, c: (b, 0, 0, 0, 0))
    cell = pl.BlockSpec((2, TILE, GW), lambda b, c: (0, b, 0))
    shape = jax.ShapeDtypeStruct((2, CELL, GW), jnp.bfloat16)
    both = pl.BlockSpec((2, 2, TILE, GW), lambda b, c: (0, 0, b, 0))
    both_shape = jax.ShapeDtypeStruct((2, 2, CELL, GW), jnp.bfloat16)
    specs, shapes = [cell, cell, both, both], [shape, shape, both_shape, both_shape]
    return merge(core, [pieces, other], merge_kernel, [piece, piece], specs, shapes)


def merge_queries(core, got):
    pieces = got.reshape(2, 2, 4, 3 * PIECE, GW)
    leaving = pieces[:, :, :, : 2 * PIECE]
    other = send(lax.dynamic_index_in_dim(leaving, 1 - core[0], 1, keepdims=False), OTHER_CORE)
    specs = [
        pl.BlockSpec((1, 1, 4, 2 * PIECE, GW), lambda b, c: (b, c[0], 0, 0, 0)),
        pl.BlockSpec((1, 4, 2 * PIECE, GW), lambda b, c: (b, 0, 0, 0)),
        pl.BlockSpec((16, PIECE, GW), lambda b, c: (0, 2, 0)),
    ]
    out_specs = [
        pl.BlockSpec((2, 1, TILE, GW), lambda b, c: (0, b, 0, 0)),
        pl.BlockSpec((3, TXT, GW), lambda b, c: (0, 0, 0)),
    ]
    shapes = [
        jax.ShapeDtypeStruct((2, 2, TILE, GW), jnp.bfloat16),
        jax.ShapeDtypeStruct((3, TXT, GW), jnp.bfloat16),
    ]
    return merge(core, [pieces, other, got], merge_queries_kernel, specs, out_specs, shapes)


def join_kernel(left_ref, right_ref, out_ref):
    out_ref[:, 0] = left_ref[...]
    out_ref[:, 1] = right_ref[...]


def join(left, right):
    half = pl.BlockSpec((1, CELL, GW), lambda k: (k, 0, 0))
    return pl.pallas_call(
        join_kernel,
        grid=(2,),
        in_specs=[half, half],
        out_specs=pl.BlockSpec((1, 2, CELL, GW), lambda k: (k, 0, 0, 0)),
        out_shape=jax.ShapeDtypeStruct((2, 2, CELL, GW), jnp.bfloat16),
        compiler_params=pltpu.CompilerParams(vmem_limit_bytes=56 * 2**20),
        cost_estimate=pl.CostEstimate(flops=0, bytes_accessed=16 * CELL * GW, transcendentals=0),
        name="join",
    )(left, right)


def project_kernel(from_ref, first, second, third, fourth, weight_ref, out_ref, whole_ref):
    @pl.when(pl.program_id(0) == 0)
    def _():
        for i, ref in enumerate((first, second, third, fourth)):
            whole_ref[:, pl.ds(pl.multiple_of(from_ref[i] * GW, GW), GW)] = ref[...]

    columns = pl.ds(pl.multiple_of(pl.program_id(0) * COLUMNS, COLUMNS), COLUMNS)
    out_ref[...] = jnp.dot(
        whole_ref[...], weight_ref[:, columns], preferred_element_type=jnp.float32
    ).astype(jnp.bfloat16)


def project(groups, parts, weight):
    depth, width = weight.shape
    part = pl.BlockSpec((TILE, GW), lambda n, groups: (0, 0))
    return pl.pallas_call(
        project_kernel,
        grid_spec=pltpu.PrefetchScalarGridSpec(
            num_scalar_prefetch=1,
            grid=(width // COLUMNS,),
            in_specs=[part] * 4 + [pl.BlockSpec(memory_space=pltpu.VMEM)],
            out_specs=pl.BlockSpec((TILE, COLUMNS), lambda n, groups: (0, n)),
            scratch_shapes=[pltpu.VMEM((TILE, depth), jnp.bfloat16)],
        ),
        out_shape=jax.ShapeDtypeStruct((TILE, width), jnp.bfloat16),
        compiler_params=pltpu.CompilerParams(vmem_limit_bytes=24 * 2**20),
        cost_estimate=pl.CostEstimate(
            flops=2 * TILE * depth * width, bytes_accessed=2 * depth * width, transcendentals=0
        ),
        name="project",
    )(groups, *parts, weight)


def wide_bias(table):
    halves = [
        jnp.broadcast_to(table[b][None], (TILE // EXTRA, EXTRA, HD)).reshape(TILE, HD)
        for b in range(2)
    ]
    return jnp.concatenate(halves)


def add_keys(query, state, keys, bias, values):
    ones = jnp.ones((keys.shape[0], HD), jnp.bfloat16)
    scores = lax.dot_general(
        query,
        jnp.concatenate([keys, bias], axis=1),
        CONTRACT_LAST,
        preferred_element_type=jnp.float32,
    )
    top = jnp.max(scores, axis=1, keepdims=True)
    if state is not None:
        top = jnp.maximum(top, state[0])
    weights = jnp.exp2((scores - top) * SCALE).astype(jnp.bfloat16)
    part = jnp.dot(
        weights, jnp.concatenate([values, ones], axis=1), preferred_element_type=jnp.float32
    )
    if state is not None:
        part = part + state[1] * jnp.exp2((state[0] - top) * SCALE)
    return top, part


def add_all(query, state, blocks):
    for keys, bias, values in blocks:
        state = add_keys(query, state, keys(), wide_bias(bias()), values())
    return state, None


def add_all_late(query, state, blocks):
    peak, total = state
    step = None
    for keys, bias, values in blocks:
        scores = lax.dot_general(
            query,
            jnp.concatenate([keys(), wide_bias(bias())], axis=1),
            CONTRACT_LAST,
            preferred_element_type=jnp.float32,
        )
        weights = jnp.exp2((scores - peak) * SCALE).astype(jnp.bfloat16)
        ones = jnp.ones((CELL, HD), jnp.bfloat16)
        part = jnp.dot(
            weights, jnp.concatenate([values(), ones], axis=1), preferred_element_type=jnp.float32
        )
        top = jnp.maximum(peak, jnp.max(scores, axis=1, keepdims=True))
        rise = top - peak
        total = (total + part) * jnp.exp2(-rise * SCALE)
        step = rise if step is None else jnp.maximum(step, rise)
        peak = top
    return (peak, total), jnp.max(step)


def widened(query, first_lane):
    rows = query.shape[0]
    lanes = lax.broadcasted_iota(jnp.int32, (rows, HD), 1)
    which = lax.broadcasted_iota(jnp.int32, (rows, HD), 0) // TILE
    hot = jnp.where(lanes == first_lane + which, 1.0, 0.0).astype(jnp.bfloat16)
    return jnp.concatenate([query, hot], axis=1)


def lanes_of(rows):
    return lax.broadcasted_iota(jnp.int32, (rows, HD), 1)


def near_kernel(cells, q_ref, tk_ref, tv_ref, bias_ref, *refs):
    sum_ref, mark_ref = refs[2 * cells :]

    def run(w, late):
        query = widened(q_ref[w].reshape(CELL, HD), 2 * w)
        no_bias = jnp.zeros((TXT, HD), jnp.bfloat16)
        state = add_keys(query, None, tk_ref[0], no_bias, tv_ref[0])
        blocks = [
            (
                functools.partial(refs[2 * (i // 2)].__getitem__, (0, i % 2)),
                functools.partial(bias_ref.__getitem__, i),
                functools.partial(refs[2 * (i // 2) + 1].__getitem__, (0, i % 2)),
            )
            for i in range(2 * cells)
        ]
        state, step = late(query, state, blocks)
        sum_ref[w] = state[1][:, :HD]
        lanes, head = lanes_of(CELL), pl.program_id(0)
        mark = jnp.where(lanes < 8, jnp.broadcast_to(state[0], (CELL, HD)), state[1][:, HD:])
        others = jnp.where(head == 0, 0.0, mark_ref[w])
        mark_ref[w] = jnp.where(lanes % 8 == head, mark, others)
        return step

    step = jnp.maximum(run(0, add_all_late), run(1, add_all_late))

    @pl.when(step > TOO_FAR)
    def _():
        @pl.loop(0, 2)
        def _(w):
            run(w, add_all)


def cell_specs(number):
    def spec(kind):
        return pl.BlockSpec((1, 2, CELL, HD), lambda h: (kind, 0, 0, h))

    return [spec(0), spec(1)] * number


def doubled(cells):
    return [array for cell in cells for array in (cell, cell)]


def cost(rows, keys, heads):
    return pl.CostEstimate(
        flops=rows * keys * heads * 4 * 384,
        bytes_accessed=4 * keys * heads * HD,
        transcendentals=rows * keys * heads,
    )


def near(queries, text_all, bias, cells):
    state = pl.BlockSpec((2, CELL, HD), lambda h: (0, 0, h))
    shape = jax.ShapeDtypeStruct((2, CELL, GW), jnp.float32)
    return pl.pallas_call(
        functools.partial(near_kernel, len(cells)),
        grid=(GH,),
        in_specs=[
            pl.BlockSpec((2, 2, TILE, HD), lambda h: (0, 0, 0, h)),
            pl.BlockSpec((1, TXT, HD), lambda h: (1, 0, h)),
            pl.BlockSpec((1, TXT, HD), lambda h: (2, 0, h)),
            pl.BlockSpec(bias.shape, lambda h: (0, 0, 0, 0)),
        ]
        + cell_specs(len(cells)),
        out_specs=[state, pl.BlockSpec((2, CELL, HD), lambda h: (0, 0, 0))],
        out_shape=[shape, jax.ShapeDtypeStruct((2, CELL, HD), jnp.float32)],
        compiler_params=pltpu.CompilerParams(vmem_limit_bytes=52 * 2**20),
        cost_estimate=cost(2 * CELL, 2 * len(cells) * CELL + TXT, GH),
        name="near_cells",
    )(queries, text_all, text_all, bias, *doubled(cells))


def side_kernel(valid_ref, q_ref, sum_ref, mark_ref, bias_ref, *refs):
    out_ref = refs[6]
    row = lax.broadcasted_iota(jnp.int32, (CELL, HD), 0)

    def run(w, late):
        query = widened(q_ref[w].reshape(CELL, HD), 2 * w)
        mark = mark_ref[w]
        lanes, head = lanes_of(CELL), pl.program_id(0)
        peak = jnp.sum(jnp.where(lanes == head, mark, 0.0), axis=1, keepdims=True)
        total = jnp.sum(jnp.where(lanes == 8 + head, mark, 0.0), axis=1, keepdims=True)
        totals = jnp.broadcast_to(total, (CELL, HD))
        state = (peak, jnp.concatenate([sum_ref[w], totals], axis=1))
        blocks = [
            (
                functools.partial(refs[2 * i].__getitem__, (0, w)),
                functools.partial(bias_ref.__getitem__, 3 * w + i),
                functools.partial(refs[2 * i + 1].__getitem__, (0, w)),
            )
            for i in range(3)
        ]
        state, step = late(query, state, blocks)
        value = state[1][:, :HD] / state[1][:, HD:]
        value = jnp.where(row % TC < valid_ref[w], value, 0.0).astype(jnp.bfloat16)
        out_ref[w] = value.reshape(2, TILE, HD)
        return step

    step = jnp.maximum(run(0, add_all_late), run(1, add_all_late))

    @pl.when(step > TOO_FAR)
    def _():
        @pl.loop(0, 2)
        def _(w):
            run(w, add_all)


def side(valid, queries, state, bias, cells):
    tall = pl.BlockSpec((2, CELL, HD), lambda h: (0, 0, h))
    query = pl.BlockSpec((2, 2, TILE, HD), lambda h: (0, 0, 0, h))
    return pl.pallas_call(
        side_kernel,
        grid=(GH,),
        in_specs=[
            pl.BlockSpec(memory_space=pltpu.SMEM),
            query,
            tall,
            pl.BlockSpec((2, CELL, HD), lambda h: (0, 0, 0)),
            pl.BlockSpec(bias.shape, lambda h: (0, 0, 0, 0)),
        ]
        + cell_specs(3),
        out_specs=query,
        out_shape=jax.ShapeDtypeStruct((2, 2, TILE, GW), jnp.bfloat16),
        compiler_params=pltpu.CompilerParams(vmem_limit_bytes=52 * 2**20),
        cost_estimate=cost(2 * CELL, 3 * CELL, GH),
        name="side_cells",
    )(valid, queries, *state, bias, *doubled(cells))


def text_kernel(share_ref, q_ref, tk_ref, tv_ref, bias_ref, *refs):
    out_ref = refs[2]
    head = pl.program_id(0)
    lanes = lax.broadcasted_iota(jnp.int32, (TXT, HD), 1)
    rows = lax.broadcasted_iota(jnp.int32, (TXT, HD), 0)
    hot = jnp.where(lanes == TEXT_LANE, 1.0, 0.0).astype(jnp.bfloat16)
    query = jnp.concatenate([q_ref[0], hot], axis=1)
    share = jnp.where(rows // 8 == share_ref[0], 0.0, MASKED).astype(jnp.bfloat16)
    state = None
    for i in range(2):
        bias = wide_bias(bias_ref[i])
        state = add_keys(query, state, refs[0][0, i], bias, refs[1][0, i])
    state = add_keys(query, state, tk_ref[0], share, tv_ref[0])
    out_ref[:, pl.ds(pl.multiple_of(head * HD, HD), HD)] = state[1][:, :HD]
    mark = jnp.where(
        lanes % 8 == head, jnp.where(lanes < 8, state[0], state[1][:, HD:]), 0.0
    )

    @pl.when(head == 0)
    def _():
        out_ref[:, GW:] = mark

    @pl.when(head > 0)
    def _():
        out_ref[:, GW:] += mark


def text_part(share, text_all, bias, cells):
    def spec(kind):
        return pl.BlockSpec((1, TXT, HD), lambda h: (kind, 0, h))

    return pl.pallas_call(
        text_kernel,
        grid=(GH,),
        in_specs=[
            pl.BlockSpec(memory_space=pltpu.SMEM),
            spec(0),
            spec(1),
            spec(2),
            pl.BlockSpec(bias.shape, lambda h: (0, 0, 0, 0)),
        ]
        + cell_specs(1),
        out_specs=pl.BlockSpec((TXT, GW + HD), lambda h: (0, 0)),
        out_shape=jax.ShapeDtypeStruct((TXT, GW + HD), jnp.float32),
        compiler_params=pltpu.CompilerParams(vmem_limit_bytes=56 * 2**20),
        cost_estimate=cost(TXT, 2 * CELL + TXT, GH),
        name="text_queries",
    )(share, text_all, text_all, text_all, bias, *doubled(cells))


def text_sum_kernel(part_ref, out_ref):
    for z in range(4):
        marks = part_ref[z, :, :, GW:]
        top = jnp.max(marks, axis=0, keepdims=True)
        factors = jnp.exp2((marks - top) * SCALE)
        for h in range(GH):
            factor = factors[..., h : h + 1]
            total = jnp.sum(marks[..., 8 + h : 9 + h] * factor, axis=0)
            part = part_ref[z, :, :, h * HD : (h + 1) * HD]
            summed = jnp.sum(part * factor, axis=0) / total
            start = z * GW + h * HD
            out_ref[:, start : start + HD] = summed.astype(jnp.bfloat16)


def text_sum(parts):
    return pl.pallas_call(
        text_sum_kernel,
        out_shape=jax.ShapeDtypeStruct((2, 4 * GW), jnp.bfloat16),
        compiler_params=pltpu.CompilerParams(vmem_limit_bytes=56 * 2**20),
        cost_estimate=pl.CostEstimate(
            flops=0, bytes_accessed=TXT * (GW + HD) * 4, transcendentals=0
        ),
        name="text_sum",
    )(parts.reshape(4, 32, 2, GW + HD))


def shards(
    video_query,
    video_key,
    video_value,
    text_query,
    text_key,
    text_value,
    window_lists,
    valid_columns,
    video_weight,
    text_weight,
):
    tm, space = lax.axis_index("tm"), lax.axis_index("space")
    y, zl = tm // 2, tm % 2
    zh, x, c = space // 8, space // 2 % 4, space % 2
    z = 2 * zh + zl
    moment = 2 * y + c

    packed = pack(pack_kernel, 4 * PIECE, [video_key, video_value])
    packed, lists = lax.optimization_barrier((packed, window_lists))
    got = exchange(packed, PLANES)

    other_lists = send(lists, TIME_PARTNER)
    text_rows = jnp.concatenate([text_query, text_key, text_value], axis=0)
    text_some = lax.all_gather(text_rows, AXES, axis_index_groups=SAME_PLACE, tiled=True)
    text_some = text_some.reshape(8, 3, 2, 4 * GW).transpose(1, 0, 2, 3).reshape(PIECE, 4 * GW)
    packed_queries = pack(pack_queries_kernel, 3 * PIECE, [video_query], text_some)
    got, packed_queries = lax.optimization_barrier((got, packed_queries))

    core = c.reshape(1)
    pieces = got.reshape(2, 2, 4, 4 * PIECE, GW)
    other = send(pieces, OTHER_CORE)
    low, high, own, beside = merge_keys(core, pieces, other)

    left, right = send(high, in_columns(1)), send(low, in_columns(-1))
    beyond = send(own, OTHER_CHIP)

    got_queries = exchange(packed_queries, PLANES)
    queries, text_all = merge_queries(core, got_queries)

    got_lists = jnp.where(zl == c, lists, other_lists).reshape(2, 8, 27)
    tile_lists = lax.dynamic_slice_in_dim(got_lists, 2 * x, 2, 1).transpose(1, 0, 2).reshape(4, 27)
    key_moment = moment + jnp.arange(-1, 2, dtype=jnp.int32)[:, None, None]
    key_column = 2 * x + jnp.arange(-1, 3, dtype=jnp.int32)[None, :, None]
    key_band = jnp.arange(2, dtype=jnp.int32)[None, None, :]
    inside = (key_moment >= 0) & (key_moment < 8) & (key_column >= 0) & (key_column < 8)
    idents = jnp.where(inside, 16 * key_moment + 8 * key_band + key_column, -2)
    listed = jnp.any(idents[..., None, None] == tile_lists, axis=-1)
    places = jnp.arange(8, dtype=jnp.int32)
    columns = 2 * x + jnp.arange(-1, 3, dtype=jnp.int32)
    valid = jnp.sum(
        jnp.where(places[None, :] == columns[:, None], valid_columns[None, :], 0), axis=1
    )
    fine = (jnp.arange(EXTRA, dtype=jnp.int32) % TC)[None, :] < valid[:, None]
    listed = jnp.pad(listed, ((0, 0), (0, 0), (0, 0), (0, HD - 4)), constant_values=True)
    allowed = listed[:, :, :, None, :] & fine[None, :, None, :, None]
    bias = jnp.where(allowed, 0.0, MASKED).astype(jnp.bfloat16)
    even_core = c == 0
    beside_bias = jnp.where(even_core, bias[2], bias[0])
    beyond_bias = jnp.where(even_core, bias[0], bias[2])
    bias = jnp.stack([bias[1], beside_bias, beyond_bias])
    near_bias = bias[:, 1:3].reshape(6, 2, EXTRA, HD)
    side_bias = jnp.concatenate([bias[:, 0], bias[:, 3]])

    member = (4 * y + x) * 2 + c
    parts = text_part(member.reshape(1), text_all, near_bias[:2], [own])
    left, right, _, queries = lax.optimization_barrier((left, right, parts, queries))
    parts = exchange(parts.reshape(128, 2, GW + HD), EVERYONE)
    sides = join(left, right)
    beside_sides, beyond_sides = send(sides, OTHER_CORE), send(sides, OTHER_CHIP)

    state = near(queries, text_all, near_bias, [own, beside, beyond])
    attended = side(valid[1:3], queries, state, side_bias, [sides, beside_sides, beyond_sides])
    parts, attended = lax.optimization_barrier((parts, attended))
    attended = attended.reshape(4, TILE, GW)

    turns = jnp.arange(4, dtype=jnp.int32)
    arrived = [
        send(lax.dynamic_index_in_dim(attended, (z + turn) % 4, 0, keepdims=False), to_owner(turn))
        for turn in range(4)
    ]
    video_output = project((2 * (x % 2) + c - turns) % 4, arrived, video_weight)
    video_output = video_output.reshape(1, 1, 1, TILE, -1)
    text_attn = text_sum(parts)
    text_output = jnp.dot(text_attn, text_weight, preferred_element_type=jnp.float32)
    text_output = text_output.astype(jnp.bfloat16)
    return (video_output, text_output)


def solution(mesh):
    in_specs = (
        P("tm", "space", None, None),
        P("tm", "space", None, None),
        P("tm", "space", None, None),
        P(("tm", "space"), None),
        P(("tm", "space"), None),
        P(("tm", "space"), None),
        P("tm", None, None),
        P(),
        P(),
        P(),
    )
    out_specs = (P("tm", "space", None, None, None), P(("tm", "space"), None))
    return jax.shard_map(shards, mesh=mesh, in_specs=in_specs, out_specs=out_specs, check_vma=False)
```
